32 devices in a mesh: groups: 2 (over x), graph: 16 (over z, y, core).
Axes of the slice: x: 2, y: 2, z: 4, core: 2. Of those that a mesh axis runs over, the one named last changes fastest.
Arguments:
- node_irreps: bfloat16 [1536, 49, 128], P(('groups', 'graph')), parts along dimension 0, may hold values from -6 to 6
- cotangent: bfloat16 [1536, 49, 128], P(('groups', 'graph')), parts along dimension 0, may hold values from -6 to 6
- rotation: bfloat16 [235, 18432], P(None, ('groups', 'graph')), parts along dimension 1, may hold values from -1.75 to 1.75
- radial: bfloat16 [18432, 128], P(('groups', 'graph')), parts along dimension 0, may hold values from -6 to 6
- edge_source: int32 [18432], P(('groups', 'graph')), parts along dimension 0, may hold values from 0 to 79, as said below
- edge_valid: int32 [18432], P(('groups', 'graph')), parts along dimension 0, may hold values 0 or 1
- send_rows: int32 [128, 8], P(('groups', 'graph')), parts along dimension 0, may hold values from 0 to 47
- w_zero: bfloat16 [896, 896], replicated, may hold values from -0.1875 to 0.1875
- w_one: bfloat16 [768, 1536], replicated, may hold values from -0.15625 to 0.15625
- w_two: bfloat16 [640, 1280], replicated, may hold values from -0.15625 to 0.15625
Outputs:
- grad_nodes: bfloat16 [1536, 49, 128], P(('groups', 'graph')), parts along dimension 0
- grad_radial: bfloat16 [18432, 128], P(('groups', 'graph')), parts along dimension 0
- grad_w_zero: float32 [1605632], P(('groups', 'graph')), parts along dimension 0
- grad_w_one: float32 [2359296], P(('groups', 'graph')), parts along dimension 0
- grad_w_two: float32 [1638400], P(('groups', 'graph')), parts along dimension 0
The draws below stay inside these ranges and needn't reach their ends.
There are 2 independent parts, one for each index of `groups`. The reference program is written for one: setup_inputs(seed, part) draws one part's arguments, and reference() takes and returns one part's arrays. A program takes and returns all parts, laid end to end along the dimension named above; an argument that names none is the same for every part. Nothing has to cross between parts.
Inputs may be any that keep to these rules, and one draw needn't show every extreme that they name: `edge_source`: A value v >= 48 names slot (v - 48) % 8 of the block that partition d - o_j sends to d, j = (v - 48) // 8; that partition exists.
All inputs are finite; a program needn't handle non-finite values. No bound on the sum of `edge_valid` on one device may be relied on, other than what follows from the above.
Results may differ from the reference program's by a relative error of at most 0.01.
Values may be sent and summed in bfloat16 or wider, within the bound.
A program may use at most 192 MiB of HBM per device.

```python
import jax
import jax.numpy as jnp
import numpy as np
from jax import lax

CH = 128
COEF = 49
PACKED = 235
NEIGH = 12
ATOMS_DEV = 48
HALO = 8
ATOMS = 768
EDGES = 9216
N_GRAPH = 16


def draw_edge_source(key, part):
    key = jax.random.fold_in(key, 11)
    key_row, key_block, key_slot, key_remote = jax.random.split(key, 4)
    per_device = ATOMS_DEV * NEIGH
    device = jnp.arange(EDGES, dtype=jnp.int32) // per_device
    local_row = jax.random.randint(key_row, (EDGES,), 0, ATOMS_DEV, dtype=jnp.int32)
    peer_block = jax.random.randint(key_block, (EDGES,), 0, 4, dtype=jnp.int32)
    slot_index = jax.random.randint(key_slot, (EDGES,), 0, HALO, dtype=jnp.int32)
    remote = jax.random.randint(key_remote, (EDGES,), 0, 5, dtype=jnp.int32) < 2
    offsets = jnp.array([-2, -1, 1, 2], jnp.int32)[peer_block]
    sender = device - offsets
    usable = remote & (sender >= 0) & (sender < N_GRAPH)
    source_code = jnp.where(usable, ATOMS_DEV + peer_block * HALO + slot_index, local_row)
    source_code = source_code.at[EDGES - 1].set(ATOMS_DEV + 4 * HALO - 1)
    source_code = source_code.at[0].set(0)
    return source_code.astype(jnp.int32)


def with_ends(drawn, own_key, low, high):
    longest = drawn.shape.index(max(drawn.shape))
    spots = []
    for shift in (0, 1):
        where = [jax.random.randint(jax.random.fold_in(own_key, axis), (), 0, length) for axis, length in enumerate(drawn.shape)]
        where[longest] = (where[longest] + shift) % drawn.shape[longest]
        spots.append(tuple(where))
    return drawn.at[spots[0]].set(low).at[spots[1]].set(high)


def levels(stream_key, shape, shards, smallest, top_value):
    level = 1.0
    for position, shards_of in shards:
        steps = jax.random.uniform(jax.random.fold_in(jax.random.fold_in(stream_key, 6), position), (shards_of,), jnp.float32, smallest / len(shards), top_value / len(shards))
        level = level * jnp.repeat(jnp.exp(steps), shape[position] // shards_of).reshape((-1,) + (1,) * (len(shape) - 1 - position))
    return level


def noise(stream_key, extent, scale, reach, pieces=(), kind=jnp.bfloat16):
    result = jax.random.normal(stream_key, extent, jnp.float32) * scale
    if len(pieces) > 0:
        result = levels(stream_key, extent, pieces, -0.22, 0.18) * result
    return jnp.clip(result, min=-reach, max=reach).astype(kind)


def setup_inputs(seed: int = 0, part: int = 0) -> dict:
    splits = jax.random.split(jax.random.key(seed), 11)
    part_splits = jax.random.split(jax.random.fold_in(splits[10], part), 11)
    return {
        "node_irreps": noise(part_splits[0], (ATOMS, COEF, CH), 1.0, 6.0, ((0, 16),)),
        "cotangent": noise(part_splits[1], (ATOMS, COEF, CH), 1.0, 6.0, ((0, 16),)),
        "rotation": noise(part_splits[2], (PACKED, EDGES), 0.3, 1.75, ((1, 16),)),
        "radial": noise(part_splits[3], (EDGES, CH), 1.0, 6.0, ((0, 16),)),
        "edge_source": draw_edge_source(jax.random.fold_in(jax.random.fold_in(splits[10], part), 71), part),
        "edge_valid": with_ends((jax.random.randint(part_splits[5], (EDGES,), 0, 4) < 3).astype(jnp.int32), jax.random.fold_in(part_splits[5], 1), 0, 1),
        "send_rows": with_ends(jax.random.randint(part_splits[6], (4 * N_GRAPH, HALO), 0, ATOMS_DEV), jax.random.fold_in(part_splits[6], 1), 0, ATOMS_DEV - 1).astype(jnp.int32),
        "w_zero": noise(splits[7], (7 * CH, 7 * CH), (7 * CH) ** -0.5, 0.1875),
        "w_one": noise(splits[8], (6 * CH, 12 * CH), (12 * CH) ** -0.5, 0.15625),
        "w_two": noise(splits[9], (5 * CH, 10 * CH), (10 * CH) ** -0.5, 0.15625),
    }


peer_steps = (-2, -1, 1, 2)


def rotation_tables():
    row_list = []
    col_list = []
    order_rows = {0: 0, 1: 6, -1: 12, 2: 17, -2: 22}
    for degree in range(7):
        orders = [0, 1, -1, 2, -2][:min(2 * degree + 1, 5)]
        for order_value in orders:
            for column_step in range(2 * degree + 1):
                row_list.append(order_rows[order_value] + degree)
                col_list.append(degree * degree + column_step)
    return np.array(row_list, np.int32), np.array(col_list, np.int32)


def split_orders(values):
    edge_count = values.shape[0]
    return (values[:, 0:7].reshape(edge_count, -1), values[:, 7:13].reshape(edge_count, -1),
            values[:, 13:19].reshape(edge_count, -1), values[:, 19:24].reshape(edge_count, -1),
            values[:, 24:29].reshape(edge_count, -1))


def times_transposed(left, weight):
    return lax.dot_general(left, weight, (((1,), (1,)), ((), ())), preferred_element_type=jnp.float32)


def contract_rows(left, right):
    return lax.dot_general(left, right, (((0,), (0,)), ((), ())), preferred_element_type=jnp.float32)


def edge_backward(gathered, cotangent, rotation, radial, edge_valid, w_zero, w_one, w_two):
    rows_table, cols_table = rotation_tables()
    edge_count, coef_count, channels = gathered.shape
    atom_count = cotangent.shape[0]
    neighbours = edge_count // atom_count
    dense = jnp.zeros((29, coef_count, edge_count), jnp.float32).at[rows_table, cols_table].set(rotation.astype(jnp.float32))
    rotated = jnp.einsum("kne,enc->ekc", dense, gathered.astype(jnp.float32))
    radial_wide = radial[:, None, :].astype(jnp.float32)
    inputs = (rotated * radial_wide).astype(jnp.bfloat16)
    dense_atoms = dense.reshape(29, coef_count, atom_count, neighbours)
    toward = jnp.einsum("knas,anc->askc", dense_atoms, cotangent.astype(jnp.float32)).reshape(edge_count, 29, channels)
    grad_out = (toward * edge_valid[:, None, None].astype(jnp.float32)).astype(jnp.bfloat16)
    in_zero, in_plus, in_minus, in_plus_two, in_minus_two = split_orders(inputs)
    out_zero, out_plus, out_minus, out_plus_two, out_minus_two = split_orders(grad_out)
    width_one = w_one.shape[0]
    first_one = w_one[:, :width_one]
    second_one = w_one[:, width_one:]
    width_two = w_two.shape[0]
    first_two = w_two[:, :width_two]
    second_two = w_two[:, width_two:]
    back_zero = times_transposed(out_zero, w_zero)
    back_plus = times_transposed(out_plus, first_one) + times_transposed(out_minus, second_one)
    back_minus = times_transposed(out_minus, first_one) - times_transposed(out_plus, second_one)
    back_plus_two = times_transposed(out_plus_two, first_two) + times_transposed(out_minus_two, second_two)
    back_minus_two = times_transposed(out_minus_two, first_two) - times_transposed(out_plus_two, second_two)
    grad_zero = contract_rows(in_zero, out_zero)
    grad_one = jnp.concatenate([contract_rows(in_plus, out_plus) + contract_rows(in_minus, out_minus),
                                contract_rows(in_plus, out_minus) - contract_rows(in_minus, out_plus)], axis=1)
    grad_two = jnp.concatenate([contract_rows(in_plus_two, out_plus_two) + contract_rows(in_minus_two, out_minus_two),
                                contract_rows(in_plus_two, out_minus_two) - contract_rows(in_minus_two, out_plus_two)], axis=1)
    grad_in = jnp.concatenate([back_zero.reshape(edge_count, 7, channels), back_plus.reshape(edge_count, 6, channels),
                               back_minus.reshape(edge_count, 6, channels), back_plus_two.reshape(edge_count, 5, channels),
                               back_minus_two.reshape(edge_count, 5, channels)], axis=1)
    grad_radial = jnp.sum(grad_in * rotated, axis=1).astype(jnp.bfloat16)
    weighted = grad_in * radial_wide
    edge_grad = jnp.einsum("kne,ekc->enc", dense, weighted, precision=lax.Precision.HIGHEST)
    return edge_grad, grad_radial, grad_zero, grad_one, grad_two


def reference(node_irreps, cotangent, rotation, radial, edge_source, edge_valid, send_rows, w_zero, w_one, w_two):
    per_device = ATOMS_DEV * NEIGH
    channels = node_irreps.shape[2]
    coef_count = node_irreps.shape[1]
    step_array = jnp.array(peer_steps, jnp.int32)
    segment_total = ATOMS_DEV + 4 * HALO

    def one_device(carry, device):
        accum, sum_zero, sum_one, sum_two = carry
        first_edge = device * per_device
        source_code = lax.dynamic_slice_in_dim(edge_source, first_edge, per_device)
        valid_piece = lax.dynamic_slice_in_dim(edge_valid, first_edge, per_device)
        rotation_piece = lax.dynamic_slice_in_dim(rotation, first_edge, per_device, 1)
        radial_piece = lax.dynamic_slice_in_dim(radial, first_edge, per_device)
        cot_piece = lax.dynamic_slice_in_dim(cotangent, device * ATOMS_DEV, ATOMS_DEV)
        is_local = source_code < ATOMS_DEV
        remote_code = jnp.clip(source_code - ATOMS_DEV, 0, 4 * HALO - 1)
        peer_block = remote_code // HALO
        slot_index = remote_code % HALO
        sender = jnp.clip(device - step_array[peer_block], 0, N_GRAPH - 1)
        remote_row = send_rows[sender * 4 + peer_block, slot_index]
        global_source = jnp.where(is_local, device * ATOMS_DEV + source_code, sender * ATOMS_DEV + remote_row).astype(jnp.int32)
        gathered = jnp.take(node_irreps, global_source, axis=0)
        edge_grad, grad_radial, grad_zero, grad_one, grad_two = edge_backward(
            gathered, cot_piece, rotation_piece, radial_piece, valid_piece, w_zero, w_one, w_two)
        summed = jax.ops.segment_sum(edge_grad.reshape(per_device, -1), source_code, num_segments=segment_total)
        local_grad = summed[:ATOMS_DEV]
        slot_grad = lax.optimization_barrier(summed[ATOMS_DEV:].astype(jnp.bfloat16)).astype(jnp.float32)
        slot_senders = device - step_array
        slot_ok = (slot_senders >= 0) & (slot_senders < N_GRAPH)
        clipped = jnp.clip(slot_senders, 0, N_GRAPH - 1)
        slot_rows = send_rows[clipped * 4 + jnp.arange(4, dtype=jnp.int32)]
        slot_targets = (clipped[:, None] * ATOMS_DEV + slot_rows).reshape(-1).astype(jnp.int32)
        slot_grad = slot_grad * jnp.repeat(slot_ok, HALO)[:, None].astype(jnp.float32)
        local_targets = (device * ATOMS_DEV + jnp.arange(ATOMS_DEV, dtype=jnp.int32)).astype(jnp.int32)
        accum = accum.at[local_targets].add(local_grad)
        accum = accum.at[slot_targets].add(slot_grad)
        return (accum, sum_zero + grad_zero, sum_one + grad_one, sum_two + grad_two), grad_radial

    start_carry = (jnp.zeros((ATOMS, coef_count * channels), jnp.float32),
                   jnp.zeros(w_zero.shape, jnp.float32), jnp.zeros(w_one.shape, jnp.float32),
                   jnp.zeros(w_two.shape, jnp.float32))
    final_carry, radial_grads = lax.scan(one_device, start_carry, jnp.arange(N_GRAPH, dtype=jnp.int32))
    accum, sum_zero, sum_one, sum_two = final_carry
    grad_nodes = (cotangent.astype(jnp.float32).reshape(ATOMS, -1) + accum).astype(jnp.bfloat16).reshape(node_irreps.shape)
    return grad_nodes, radial_grads.reshape(EDGES, channels), sum_zero.reshape(-1), sum_one.reshape(-1), sum_two.reshape(-1)
```

```python
import functools

import jax
import jax.numpy as jnp
from jax import lax
from jax.experimental import pallas as pl
from jax.experimental.pallas import tpu as pltpu
from jax.sharding import PartitionSpec as P

BF = jnp.bfloat16
F32 = jnp.float32
peer_steps = (-2, -1, 1, 2)
order_first = (0, 6, 12, 17, 22)
CB = 32
VMEM_LIMIT = 58 * 2**20


def degrees():
    entry = 0
    for degree in range(7):
        held = min(2 * degree + 1, 5)
        yield degree, held, entry
        entry += held * (2 * degree + 1)


def shifted(block, distance):
    devices = range(lax.axis_size("graph"))
    route = [(i - distance, i) for i in devices if i - distance in devices]
    return lax.ppermute(block, "graph", route)


def dot(left, right):
    return jnp.dot(left, right, preferred_element_type=F32)


def dot_nt(left, right):
    return lax.dot_general(left, right, (((1,), (1,)), ((), ())), preferred_element_type=F32)


def dot_tn(left, right):
    return lax.dot_general(left, right, (((0,), (0,)), ((), ())), preferred_element_type=F32)


def rows(first, count):
    return pl.ds(pl.multiple_of(first, CB), count)


def forward_kernel(
    neigh, ch, widths,
    tab_ref, cot_ref, rot_ref, rad_ref, src_ref, valid_ref,
    gz_ref, g1_ref, g2_ref, rotated_ref, gout_ref,
    xg, cx, inp, rot32, radt,
):
    coefs, slots, _ = tab_ref.shape
    atoms = cot_ref.shape[1]
    ep = rot_ref.shape[1]
    hot = (lax.broadcasted_iota(jnp.int32, (slots, ep), 0) == src_ref[...]).astype(F32).astype(BF)
    edge = lax.broadcasted_iota(jnp.int32, (atoms, ep), 1)
    first = lax.broadcasted_iota(jnp.int32, (atoms, ep), 0) * neigh
    mine = (edge >= first) & (edge < first + neigh) & (valid_ref[...] != 0)
    rep = mine.astype(F32).astype(BF)
    rot32[...] = rot_ref[...].astype(F32)
    radt[...] = rad_ref[...].astype(F32).T

    def gather(n, _):
        at = pl.ds(pl.multiple_of(n * ch, ch), ch)
        xg[at, :] = dot_tn(tab_ref[n], hot).astype(BF)
        cx[at, :] = dot_tn(cot_ref[n], rep).astype(BF)
        return _

    lax.fori_loop(0, coefs, gather, 0)

    def rotate(step, _):
        eb = step // (ch // CB)
        cb = (step % (ch // CB)) * CB
        lanes = pl.ds(pl.multiple_of(eb * 128, 128), 128)
        rad = radt[rows(cb, CB), lanes]
        for degree, held, entry in degrees():
            acc = [None] * held
            accg = [None] * held
            for j in range(2 * degree + 1):
                at = rows((degree * degree + j) * ch + cb, CB)
                x = xg[at, lanes].astype(F32)
                g = cx[at, lanes].astype(F32)
                for m in range(held):
                    k = entry + m * (2 * degree + 1) + j
                    r = rot32[k : k + 1, lanes]
                    acc[m] = r * x if j == 0 else acc[m] + r * x
                    accg[m] = r * g if j == 0 else accg[m] + r * g
            for m in range(held):
                at = rows((order_first[m] + degree) * ch + cb, CB)
                rotated_ref[at, lanes] = acc[m].astype(BF)
                inp[at, lanes] = (acc[m] * rad).astype(BF)
                gout_ref[at, lanes] = accg[m].astype(BF)
        return _

    lax.fori_loop(0, (ep // 128) * (ch // CB), rotate, 0)

    wz, w1, w2 = widths
    half = wz // 2

    def zero_part(i, _):
        at = rows(i * half, half)
        gz_ref[at, :] = dot_nt(inp[at, :], gout_ref[0:wz, :]).astype(gz_ref.dtype)
        return _

    lax.fori_loop(0, 2, zero_part, 0)
    for width, base, out in ((w1, wz, g1_ref), (w2, wz + 2 * w1, g2_ref)):
        tile = width // 2
        plus = gout_ref.at[base : base + width]
        minus = gout_ref.at[base + width : base + 2 * width]

        def pair_part(i, _, width=width, base=base, out=out, tile=tile, plus=plus, minus=minus):
            p = inp[rows(base + i * tile, tile), :]
            m = inp[rows(base + width + i * tile, tile), :]
            at = rows(i * tile, tile)
            out[at, 0:width] = (dot_nt(p, plus[...]) + dot_nt(m, minus[...])).astype(out.dtype)
            out[at, width : 2 * width] = (dot_nt(p, minus[...]) - dot_nt(m, plus[...])).astype(out.dtype)
            return _

        lax.fori_loop(0, 2, pair_part, 0)


def backward_kernel(
    ch, widths,
    rot_ref, rad_ref, src_ref, gout_ref, rotated_ref, w0_ref, w1_ref, w2_ref,
    sum_ref, grad_ref,
    gin, eg, rot32, radt, grt,
):
    coefs, slots, _ = sum_ref.shape
    ep = rot_ref.shape[1]
    edges = grad_ref.shape[0]
    hot = (lax.broadcasted_iota(jnp.int32, (slots, ep), 0) == src_ref[...]).astype(F32).astype(BF)
    rot32[...] = rot_ref[...].astype(F32)
    radt[...] = rad_ref[...].astype(F32).T
    wz, w1, w2 = widths
    half = wz // 2

    def zero_part(i, _):
        at = rows(i * half, half)
        gin[at, :] = dot(w0_ref[at, :], gout_ref[0:wz, :])
        return _

    lax.fori_loop(0, 2, zero_part, 0)
    for width, base, w_ref in ((w1, wz, w1_ref), (w2, wz + 2 * w1, w2_ref)):
        tile = width // 2
        plus = gout_ref.at[base : base + width]
        minus = gout_ref.at[base + width : base + 2 * width]

        def pair_part(i, _, width=width, base=base, w_ref=w_ref, tile=tile, plus=plus, minus=minus):
            at = rows(i * tile, tile)
            a = w_ref[at, 0:width]
            b = w_ref[at, width : 2 * width]
            gin[rows(base + i * tile, tile), :] = dot(a, plus[...]) + dot(b, minus[...])
            gin[rows(base + width + i * tile, tile), :] = dot(a, minus[...]) - dot(b, plus[...])
            return _

        lax.fori_loop(0, 2, pair_part, 0)

    def rotate(step, _):
        eb = step // (ch // CB)
        cb = (step % (ch // CB)) * CB
        lanes = pl.ds(pl.multiple_of(eb * 128, 128), 128)
        rad = radt[rows(cb, CB), lanes]
        total = jnp.zeros((CB, 128), F32)
        for degree, held, entry in degrees():
            weighted = []
            for m in range(held):
                at = rows((order_first[m] + degree) * ch + cb, CB)
                value = gin[at, lanes]
                total = total + value * rotated_ref[at, lanes].astype(F32)
                weighted.append(value * rad)
            for j in range(2 * degree + 1):
                acc = None
                for m in range(held):
                    k = entry + m * (2 * degree + 1) + j
                    term = rot32[k : k + 1, lanes] * weighted[m]
                    acc = term if m == 0 else acc + term
                eg[rows((degree * degree + j) * ch + cb, CB), lanes] = acc.astype(BF)
        grt[rows(cb, CB), lanes] = total
        return _

    lax.fori_loop(0, (ep // 128) * (ch // CB), rotate, 0)
    grad_ref[...] = grt[...].T[:edges].astype(BF)

    def scatter(i, _):
        part = dot_nt(hot, eg[pl.ds(pl.multiple_of(i * 7 * ch, ch), 7 * ch), :])
        for j in range(7):
            sum_ref[i * 7 + j] = part[:, j * ch : (j + 1) * ch]
        return _

    lax.fori_loop(0, coefs // 7, scatter, 0)


def body(node_irreps, cotangent, rotation, radial, edge_source, edge_valid, send_rows, w_zero, w_one, w_two):
    atoms, coefs, ch = node_irreps.shape
    halo = send_rows.shape[1]
    edges = edge_source.shape[0]
    neigh = edges // atoms
    ep = -(-edges // 128) * 128
    pad = ep - edges
    slots = atoms + 4 * halo
    widths = (w_zero.shape[0], w_one.shape[0], w_two.shape[0])
    feats = widths[0] + 2 * widths[1] + 2 * widths[2]
    send_hot = (send_rows.reshape(-1)[:, None] == jnp.arange(atoms, dtype=jnp.int32)[None, :]).astype(BF)
    nodes = node_irreps.transpose(1, 0, 2)
    cots = cotangent.transpose(1, 0, 2)
    outgoing = jnp.einsum("sa,nac->nsc", send_hot, nodes, preferred_element_type=F32).astype(BF)
    incoming = [shifted(outgoing[:, i * halo : (i + 1) * halo], peer_steps[i]) for i in range(4)]
    table = jnp.concatenate([nodes, *incoming], axis=1)
    rot = jnp.pad(rotation, ((0, 0), (0, pad)))
    rad = jnp.pad(radial, ((0, pad), (0, 0)))
    src = jnp.pad(edge_source, (0, pad), constant_values=-1)[None, :]
    valid = jnp.pad(edge_valid, (0, pad))[None, :]
    packed = rotation.shape[0]
    params = pltpu.CompilerParams(vmem_limit_bytes=VMEM_LIMIT)
    whole = pl.BlockSpec(memory_space=pltpu.VMEM)
    gz, g1, g2, rotated, gout = pl.pallas_call(
        functools.partial(forward_kernel, neigh, ch, widths),
        out_shape=(
            jax.ShapeDtypeStruct(w_zero.shape, BF),
            jax.ShapeDtypeStruct(w_one.shape, BF),
            jax.ShapeDtypeStruct(w_two.shape, BF),
            jax.ShapeDtypeStruct((feats, ep), BF),
            jax.ShapeDtypeStruct((feats, ep), BF),
        ),
        in_specs=[whole] * 6,
        out_specs=[whole] * 5,
        scratch_shapes=[
            pltpu.VMEM((coefs * ch, ep), BF),
            pltpu.VMEM((coefs * ch, ep), BF),
            pltpu.VMEM((feats, ep), BF),
            pltpu.VMEM((packed, ep), F32),
            pltpu.VMEM((ch, ep), F32),
        ],
        compiler_params=params,
        name="forward",
    )(table, cots, rot, rad, src, valid)
    grads = [
        lax.psum_scatter(g.reshape(-1), "graph", scatter_dimension=0, tiled=True).astype(F32)
        for g in (gz, g1, g2)
    ]
    summed, grad_radial = pl.pallas_call(
        functools.partial(backward_kernel, ch, widths),
        out_shape=(
            jax.ShapeDtypeStruct((coefs, slots, ch), F32),
            jax.ShapeDtypeStruct((edges, ch), BF),
        ),
        in_specs=[whole] * 8,
        out_specs=[whole] * 2,
        scratch_shapes=[
            pltpu.VMEM((feats, ep), F32),
            pltpu.VMEM((coefs * ch, ep), BF),
            pltpu.VMEM((packed, ep), F32),
            pltpu.VMEM((ch, ep), F32),
            pltpu.VMEM((ch, ep), F32),
        ],
        compiler_params=params,
        cost_estimate=pl.CostEstimate(flops=8_000_000_000, bytes_accessed=20_000_000, transcendentals=0),
        name="backward",
    )(rot, rad, src, gout, rotated, w_zero, w_one, w_two)
    slot_grad = summed[:, atoms:].astype(BF)
    returned = jnp.concatenate(
        [shifted(slot_grad[:, i * halo : (i + 1) * halo], -peer_steps[i]) for i in range(4)], axis=1
    )
    added = jnp.einsum("sa,nsc->nac", send_hot, returned, preferred_element_type=F32)
    total = cots.astype(F32) + summed[:, :atoms] + added
    grad_nodes = total.astype(BF).transpose(1, 0, 2)
    return (grad_nodes, grad_radial, *grads)


def solution(mesh):
    both = ("groups", "graph")
    return jax.shard_map(
        body,
        mesh=mesh,
        in_specs=(
            P(both, None, None), P(both, None, None), P(None, both), P(both, None),
            P(both), P(both), P(both, None), P(), P(), P(),
        ),
        out_specs=(P(both, None, None), P(both, None), P(both), P(both), P(both)),
        check_vma=False,
    )
```

```python
import functools

import jax
import jax.numpy as jnp
from jax import lax
from jax.experimental import pallas as pl
from jax.experimental.pallas import tpu as pltpu
from jax.sharding import PartitionSpec as P

BF = jnp.bfloat16
F32 = jnp.float32
peer_steps = (-2, -1, 1, 2)
order_first = (0, 6, 12, 17, 22)
CB = 32
VMEM_LIMIT = 58 * 2**20


def degrees():
    entry = 0
    for degree in range(7):
        held = min(2 * degree + 1, 5)
        yield degree, held, entry
        entry += held * (2 * degree + 1)


def shifted(block, distance):
    devices = range(lax.axis_size("graph"))
    route = [(i - distance, i) for i in devices if i - distance in devices]
    return lax.ppermute(block, "graph", route)


def dot(left, right):
    return jnp.dot(left, right, preferred_element_type=F32)


def dot_nt(left, right):
    return lax.dot_general(left, right, (((1,), (1,)), ((), ())), preferred_element_type=F32)


def dot_tn(left, right):
    return lax.dot_general(left, right, (((0,), (0,)), ((), ())), preferred_element_type=F32)


def rows(first, count):
    return pl.ds(pl.multiple_of(first, CB), count)


def forward_kernel(
    neigh, ch, widths,
    tab_ref, cot_ref, rot_ref, rad_ref, src_ref, valid_ref,
    gz_ref, g1_ref, g2_ref, rotated_ref, gout_ref,
    xg, cx, inp, rot32, radt,
):
    coefs, slots, _ = tab_ref.shape
    atoms = cot_ref.shape[1]
    ep = rot_ref.shape[1]
    hot = (lax.broadcasted_iota(jnp.int32, (slots, ep), 0) == src_ref[...]).astype(F32).astype(BF)
    edge = lax.broadcasted_iota(jnp.int32, (atoms, ep), 1)
    first = lax.broadcasted_iota(jnp.int32, (atoms, ep), 0) * neigh
    mine = (edge >= first) & (edge < first + neigh) & (valid_ref[...] != 0)
    rep = mine.astype(F32).astype(BF)
    rot32[...] = rot_ref[...].astype(F32)
    radt[...] = rad_ref[...].astype(F32).T

    def gather(n, _):
        at = pl.ds(pl.multiple_of(n * ch, ch), ch)
        xg[at, :] = dot_tn(tab_ref[n], hot).astype(BF)
        cx[at, :] = dot_tn(cot_ref[n], rep).astype(BF)
        return _

    lax.fori_loop(0, coefs, gather, 0)

    def rotate(step, _):
        eb = step // (ch // CB)
        cb = (step % (ch // CB)) * CB
        lanes = pl.ds(pl.multiple_of(eb * 128, 128), 128)
        rad = radt[rows(cb, CB), lanes]
        for degree, held, entry in degrees():
            acc = [None] * held
            accg = [None] * held
            for j in range(2 * degree + 1):
                at = rows((degree * degree + j) * ch + cb, CB)
                x = xg[at, lanes].astype(F32)
                g = cx[at, lanes].astype(F32)
                for m in range(held):
                    k = entry + m * (2 * degree + 1) + j
                    r = rot32[k : k + 1, lanes]
                    acc[m] = r * x if j == 0 else acc[m] + r * x
                    accg[m] = r * g if j == 0 else accg[m] + r * g
            for m in range(held):
                at = rows((order_first[m] + degree) * ch + cb, CB)
                rotated_ref[at, lanes] = acc[m].astype(BF)
                inp[at, lanes] = (acc[m] * rad).astype(BF)
                gout_ref[at, lanes] = accg[m].astype(BF)
        return _

    lax.fori_loop(0, (ep // 128) * (ch // CB), rotate, 0)

    wz, w1, w2 = widths
    half = wz // 2

    def zero_part(i, _):
        at = rows(i * half, half)
        gz_ref[at, :] = dot_nt(inp[at, :], gout_ref[0:wz, :]).astype(gz_ref.dtype)
        return _

    lax.fori_loop(0, 2, zero_part, 0)
    for width, base, out in ((w1, wz, g1_ref), (w2, wz + 2 * w1, g2_ref)):
        tile = width // 2
        plus = gout_ref.at[base : base + width]
        minus = gout_ref.at[base + width : base + 2 * width]

        def pair_part(i, _, width=width, base=base, out=out, tile=tile, plus=plus, minus=minus):
            p = inp[rows(base + i * tile, tile), :]
            m = inp[rows(base + width + i * tile, tile), :]
            at = rows(i * tile, tile)
            out[at, 0:width] = (dot_nt(p, plus[...]) + dot_nt(m, minus[...])).astype(out.dtype)
            out[at, width : 2 * width] = (dot_nt(p, minus[...]) - dot_nt(m, plus[...])).astype(out.dtype)
            return _

        lax.fori_loop(0, 2, pair_part, 0)


def backward_kernel(
    ch, widths,
    rot_ref, rad_ref, src_ref, gout_ref, rotated_ref, w0_ref, w1_ref, w2_ref,
    sum_ref, grad_ref,
    gin, eg, rot32, radt, grt,
):
    coefs, slots, _ = sum_ref.shape
    ep = rot_ref.shape[1]
    edges = grad_ref.shape[0]
    hot = (lax.broadcasted_iota(jnp.int32, (slots, ep), 0) == src_ref[...]).astype(F32).astype(BF)
    rot32[...] = rot_ref[...].astype(F32)
    radt[...] = rad_ref[...].astype(F32).T
    wz, w1, w2 = widths
    half = wz // 2

    def zero_part(i, _):
        at = rows(i * half, half)
        gin[at, :] = dot(w0_ref[at, :], gout_ref[0:wz, :])
        return _

    lax.fori_loop(0, 2, zero_part, 0)
    for width, base, w_ref in ((w1, wz, w1_ref), (w2, wz + 2 * w1, w2_ref)):
        tile = width // 2
        plus = gout_ref.at[base : base + width]
        minus = gout_ref.at[base + width : base + 2 * width]

        def pair_part(i, _, width=width, base=base, w_ref=w_ref, tile=tile, plus=plus, minus=minus):
            at = rows(i * tile, tile)
            a = w_ref[at, 0:width]
            b = w_ref[at, width : 2 * width]
            gin[rows(base + i * tile, tile), :] = dot(a, plus[...]) + dot(b, minus[...])
            gin[rows(base + width + i * tile, tile), :] = dot(a, minus[...]) - dot(b, plus[...])
            return _

        lax.fori_loop(0, 2, pair_part, 0)

    def rotate(step, _):
        eb = step // (ch // CB)
        cb = (step % (ch // CB)) * CB
        lanes = pl.ds(pl.multiple_of(eb * 128, 128), 128)
        rad = radt[rows(cb, CB), lanes]
        total = jnp.zeros((CB, 128), F32)
        for degree, held, entry in degrees():
            weighted = []
            for m in range(held):
                at = rows((order_first[m] + degree) * ch + cb, CB)
                value = gin[at, lanes]
                total = total + value * rotated_ref[at, lanes].astype(F32)
                weighted.append(value * rad)
            for j in range(2 * degree + 1):
                acc = None
                for m in range(held):
                    k = entry + m * (2 * degree + 1) + j
                    term = rot32[k : k + 1, lanes] * weighted[m]
                    acc = term if m == 0 else acc + term
                eg[rows((degree * degree + j) * ch + cb, CB), lanes] = acc.astype(BF)
        grt[rows(cb, CB), lanes] = total
        return _

    lax.fori_loop(0, (ep // 128) * (ch // CB), rotate, 0)
    grad_ref[...] = grt[...].T[:edges].astype(BF)

    def scatter(i, _):
        part = dot_nt(hot, eg[pl.ds(pl.multiple_of(i * 7 * ch, ch), 7 * ch), :])
        for j in range(7):
            sum_ref[i * 7 + j] = part[:, j * ch : (j + 1) * ch]
        return _

    lax.fori_loop(0, coefs // 7, scatter, 0)


def fused_kernel(
    neigh, ch, widths, graph,
    tab_ref, cot_ref, rot_ref, rad_ref, src_ref, valid_ref, w0_ref, w1_ref, w2_ref,
    sum_ref, grad_ref, oz_ref, o1_ref, o2_ref,
    xg, cx, inp, gout, rotated, rot32, radt, grt, *rest,
):
    staged = rest[0:3]
    landed = (rest[3:7], rest[7:11], rest[11:15])
    send_sem, recv_sem = rest[15], rest[16]
    outs = (oz_ref, o1_ref, o2_ref)
    me = lax.axis_index("graph")
    bits = [me & 1, (me >> 1) & 1, (me >> 2) & 1, (me >> 3) & 1]
    partners = [me + (1 << b) * (1 - 2 * bits[b]) for b in range(4)]
    barrier = pltpu.get_barrier_semaphore()
    for partner in partners:
        pl.semaphore_signal(barrier, inc=1, device_id={"graph": partner}, device_id_type=pl.DeviceIdType.MESH)

    firsts = [0]
    for stage in range(4):
        firsts.append(firsts[-1] + bits[stage] * (8 >> stage))

    def copy_of(which, stage):
        count = 8 >> stage
        at = firsts[stage] + (1 - bits[stage]) * count
        return pltpu.make_async_remote_copy(
            src_ref=staged[which].at[pl.ds(at, count)],
            dst_ref=landed[which][stage],
            send_sem=send_sem.at[which * 4 + stage],
            recv_sem=recv_sem.at[which * 4 + stage],
            device_id={"graph": partners[stage]},
            device_id_type=pl.DeviceIdType.MESH,
        )

    def advance(which, stage):
        copy_of(which, stage).wait_recv()
        count = 8 >> stage
        if stage == 3:
            outs[which][...] = staged[which][firsts[4]].astype(F32) + landed[which][3][0].astype(F32)
            return
        buffer, part, first = staged[which], landed[which][stage], firsts[stage + 1]

        def add(i, _):
            buffer[first + i] = (buffer[first + i].astype(F32) + part[i].astype(F32)).astype(BF)
            return _

        lax.fori_loop(0, count, add, 0)
        copy_of(which, stage + 1).start()

    coefs, slots, _ = tab_ref.shape
    atoms = cot_ref.shape[1]
    ep = rot_ref.shape[1]
    edges = grad_ref.shape[0]
    wz, w1, w2 = widths
    hot = (lax.broadcasted_iota(jnp.int32, (slots, ep), 0) == src_ref[...]).astype(F32).astype(BF)
    edge = lax.broadcasted_iota(jnp.int32, (atoms, ep), 1)
    first_edge = lax.broadcasted_iota(jnp.int32, (atoms, ep), 0) * neigh
    mine = (edge >= first_edge) & (edge < first_edge + neigh) & (valid_ref[...] != 0)
    rep = mine.astype(F32).astype(BF)
    rot32[...] = rot_ref[...].astype(F32)
    radt[...] = rad_ref[...].astype(F32).T

    def gather(n, _):
        at = pl.ds(pl.multiple_of(n * ch, ch), ch)
        xg[at, :] = dot_tn(tab_ref[n], hot).astype(BF)
        cx[at, :] = dot_tn(cot_ref[n], rep).astype(BF)
        return _

    lax.fori_loop(0, coefs, gather, 0)

    def rotate(step, _):
        eb = step // (ch // CB)
        cb = (step % (ch // CB)) * CB
        lanes = pl.ds(pl.multiple_of(eb * 128, 128), 128)
        rad = radt[rows(cb, CB), lanes]
        for degree, held, entry in degrees():
            acc = [None] * held
            accg = [None] * held
            for j in range(2 * degree + 1):
                at = rows((degree * degree + j) * ch + cb, CB)
                x = xg[at, lanes].astype(F32)
                g = cx[at, lanes].astype(F32)
                for m in range(held):
                    k = entry + m * (2 * degree + 1) + j
                    r = rot32[k : k + 1, lanes]
                    acc[m] = r * x if j == 0 else acc[m] + r * x
                    accg[m] = r * g if j == 0 else accg[m] + r * g
            for m in range(held):
                at = rows((order_first[m] + degree) * ch + cb, CB)
                rotated[at, lanes] = acc[m].astype(BF)
                inp[at, lanes] = (acc[m] * rad).astype(BF)
                gout[at, lanes] = accg[m].astype(BF)
        return _

    lax.fori_loop(0, (ep // 128) * (ch // CB), rotate, 0)

    def place(which, i, columns, value):
        height = value.shape[0] // 8
        for jj in range(8):
            position = (jj & 1) * 8 + ((jj >> 1) & 1) * 4 + ((jj >> 2) & 1) * 2 + i
            staged[which][position, :, columns] = value[jj * height : (jj + 1) * height].astype(BF)

    def weight_zero():
        half = wz // 2

        def part(i, _):
            place(0, i, slice(0, wz), dot_nt(inp[rows(i * half, half), :], gout[0:wz, :]))
            return _

        lax.fori_loop(0, 2, part, 0)

    def weight_pair(which, width, base):
        tile = width // 2
        plus = gout.at[base : base + width]
        minus = gout.at[base + width : base + 2 * width]

        def part(i, _):
            p = inp[rows(base + i * tile, tile), :]
            m = inp[rows(base + width + i * tile, tile), :]
            place(which, i, slice(0, width), dot_nt(p, plus[...]) + dot_nt(m, minus[...]))
            place(which, i, slice(width, 2 * width), dot_nt(p, minus[...]) - dot_nt(m, plus[...]))
            return _

        lax.fori_loop(0, 2, part, 0)

    gin = cx

    def back_zero():
        half = wz // 2

        def part(i, _):
            at = rows(i * half, half)
            gin[at, :] = dot(w0_ref[at, :], gout[0:wz, :]).astype(BF)
            return _

        lax.fori_loop(0, 2, part, 0)

    def back_pair(width, base, w_ref):
        tile = width // 2
        plus = gout.at[base : base + width]
        minus = gout.at[base + width : base + 2 * width]

        def part(i, _):
            at = rows(i * tile, tile)
            a = w_ref[at, 0:width]
            b = w_ref[at, width : 2 * width]
            gin[rows(base + i * tile, tile), :] = (dot(a, plus[...]) + dot(b, minus[...])).astype(BF)
            gin[rows(base + width + i * tile, tile), :] = (dot(a, minus[...]) - dot(b, plus[...])).astype(BF)
            return _

        lax.fori_loop(0, 2, part, 0)

    weight_pair(1, w1, wz)
    pl.semaphore_wait(barrier, 4)
    copy_of(1, 0).start()
    weight_pair(2, w2, wz + 2 * w1)
    copy_of(2, 0).start()
    advance(1, 0)
    weight_zero()
    copy_of(0, 0).start()
    advance(2, 0)
    back_zero()
    advance(0, 0)
    back_pair(w1, wz, w1_ref)
    advance(1, 1)
    back_pair(w2, wz + 2 * w1, w2_ref)

    eg = xg

    def rotate_back(step, _):
        eb = step // (ch // CB)
        cb = (step % (ch // CB)) * CB
        lanes = pl.ds(pl.multiple_of(eb * 128, 128), 128)
        rad = radt[rows(cb, CB), lanes]
        total = jnp.zeros((CB, 128), F32)
        for degree, held, entry in degrees():
            weighted = []
            for m in range(held):
                at = rows((order_first[m] + degree) * ch + cb, CB)
                value = gin[at, lanes].astype(F32)
                total = total + value * rotated[at, lanes].astype(F32)
                weighted.append(value * rad)
            for j in range(2 * degree + 1):
                acc = None
                for m in range(held):
                    k = entry + m * (2 * degree + 1) + j
                    term = rot32[k : k + 1, lanes] * weighted[m]
                    acc = term if m == 0 else acc + term
                eg[rows((degree * degree + j) * ch + cb, CB), lanes] = acc.astype(BF)
        grt[rows(cb, CB), lanes] = total
        return _

    steps = (ep // 128) * (ch // CB)
    lax.fori_loop(0, steps // 2, rotate_back, 0)
    advance(2, 1)
    advance(1, 2)
    lax.fori_loop(steps // 2, steps, rotate_back, 0)
    advance(0, 1)
    advance(2, 2)
    grad_ref[...] = grt[...].T[:edges].astype(BF)

    def scatter(i, _):
        part = dot_nt(hot, eg[pl.ds(pl.multiple_of(i * 7 * ch, ch), 7 * ch), :])
        for j in range(7):
            sum_ref[i * 7 + j] = part[:, j * ch : (j + 1) * ch]
        return _

    lax.fori_loop(0, coefs // 7, scatter, 0)
    advance(1, 3)
    advance(0, 2)
    advance(2, 3)
    advance(0, 3)
    for which in range(3):
        for stage in range(4):
            copy_of(which, stage).wait_send()


def fused(neigh, ch, widths, graph, table, cots, rot, rad, src, valid, weights, edges):
    coefs, slots, _ = table.shape
    packed, ep = rot.shape
    feats = widths[0] + 2 * widths[1] + 2 * widths[2]
    whole = pl.BlockSpec(memory_space=pltpu.VMEM)
    parts = [(w.shape[0] // graph, w.shape[1]) for w in weights]
    scratch = [
        pltpu.VMEM((coefs * ch, ep), BF),
        pltpu.VMEM((coefs * ch, ep), BF),
        pltpu.VMEM((feats, ep), BF),
        pltpu.VMEM((feats, ep), BF),
        pltpu.VMEM((feats, ep), BF),
        pltpu.VMEM((packed, ep), F32),
        pltpu.VMEM((ch, ep), F32),
        pltpu.VMEM((ch, ep), F32),
    ]
    scratch += [pltpu.VMEM((graph, *part), BF) for part in parts]
    scratch += [pltpu.VMEM((8 >> stage, *part), BF) for part in parts for stage in range(4)]
    scratch += [pltpu.SemaphoreType.DMA((12,)), pltpu.SemaphoreType.DMA((12,))]
    return pl.pallas_call(
        functools.partial(fused_kernel, neigh, ch, widths, graph),
        out_shape=(
            jax.ShapeDtypeStruct((coefs, slots, ch), F32),
            jax.ShapeDtypeStruct((edges, ch), BF),
            *(jax.ShapeDtypeStruct(part, F32) for part in parts),
        ),
        in_specs=[whole] * 9,
        out_specs=[whole] * 5,
        scratch_shapes=scratch,
        compiler_params=pltpu.CompilerParams(
            vmem_limit_bytes=VMEM_LIMIT, collective_id=0, has_side_effects=True
        ),
        name="fused",
    )(table, cots, rot, rad, src, valid, *weights)


def apart(neigh, ch, widths, table, cots, rot, rad, src, valid, weights, edges):
    w_zero, w_one, w_two = weights
    coefs, slots, _ = table.shape
    packed, ep = rot.shape
    feats = widths[0] + 2 * widths[1] + 2 * widths[2]
    params = pltpu.CompilerParams(vmem_limit_bytes=VMEM_LIMIT)
    whole = pl.BlockSpec(memory_space=pltpu.VMEM)
    gz, g1, g2, rotated, gout = pl.pallas_call(
        functools.partial(forward_kernel, neigh, ch, widths),
        out_shape=(
            jax.ShapeDtypeStruct(w_zero.shape, BF),
            jax.ShapeDtypeStruct(w_one.shape, BF),
            jax.ShapeDtypeStruct(w_two.shape, BF),
            jax.ShapeDtypeStruct((feats, ep), BF),
            jax.ShapeDtypeStruct((feats, ep), BF),
        ),
        in_specs=[whole] * 6,
        out_specs=[whole] * 5,
        scratch_shapes=[
            pltpu.VMEM((coefs * ch, ep), BF),
            pltpu.VMEM((coefs * ch, ep), BF),
            pltpu.VMEM((feats, ep), BF),
            pltpu.VMEM((packed, ep), F32),
            pltpu.VMEM((ch, ep), F32),
        ],
        compiler_params=params,
        name="forward",
    )(table, cots, rot, rad, src, valid)
    grads = [
        lax.psum_scatter(g.reshape(-1), "graph", scatter_dimension=0, tiled=True).astype(F32)
        for g in (gz, g1, g2)
    ]
    summed, grad_radial = pl.pallas_call(
        functools.partial(backward_kernel, ch, widths),
        out_shape=(
            jax.ShapeDtypeStruct((coefs, slots, ch), F32),
            jax.ShapeDtypeStruct((edges, ch), BF),
        ),
        in_specs=[whole] * 8,
        out_specs=[whole] * 2,
        scratch_shapes=[
            pltpu.VMEM((feats, ep), F32),
            pltpu.VMEM((coefs * ch, ep), BF),
            pltpu.VMEM((packed, ep), F32),
            pltpu.VMEM((ch, ep), F32),
            pltpu.VMEM((ch, ep), F32),
        ],
        compiler_params=params,
        cost_estimate=pl.CostEstimate(flops=8_000_000_000, bytes_accessed=20_000_000, transcendentals=0),
        name="backward",
    )(rot, rad, src, gout, rotated, w_zero, w_one, w_two)
    return (summed, grad_radial, *grads)


def body(node_irreps, cotangent, rotation, radial, edge_source, edge_valid, send_rows, w_zero, w_one, w_two):
    atoms, coefs, ch = node_irreps.shape
    halo = send_rows.shape[1]
    edges = edge_source.shape[0]
    neigh = edges // atoms
    ep = -(-edges // 128) * 128
    pad = ep - edges
    slots = atoms + 4 * halo
    widths = (w_zero.shape[0], w_one.shape[0], w_two.shape[0])
    feats = widths[0] + 2 * widths[1] + 2 * widths[2]
    send_hot = (send_rows.reshape(-1)[:, None] == jnp.arange(atoms, dtype=jnp.int32)[None, :]).astype(BF)
    nodes = node_irreps.transpose(1, 0, 2)
    cots = cotangent.transpose(1, 0, 2)
    outgoing = jnp.einsum("sa,nac->nsc", send_hot, nodes, preferred_element_type=F32).astype(BF)
    incoming = [shifted(outgoing[:, i * halo : (i + 1) * halo], peer_steps[i]) for i in range(4)]
    table = jnp.concatenate([nodes, *incoming], axis=1)
    rot = jnp.pad(rotation, ((0, 0), (0, pad)))
    rad = jnp.pad(radial, ((0, pad), (0, 0)))
    src = jnp.pad(edge_source, (0, pad), constant_values=-1)[None, :]
    valid = jnp.pad(edge_valid, (0, pad))[None, :]
    weights = (w_zero, w_one, w_two)
    graph = lax.axis_size("graph")
    if graph == 16 and all(w.shape[0] % (8 * graph) == 0 for w in weights):
        summed, grad_radial, *grads = fused(
            neigh, ch, widths, graph, table, cots, rot, rad, src, valid, weights, edges
        )
        grads = [g.reshape(-1) for g in grads]
    else:
        summed, grad_radial, *grads = apart(neigh, ch, widths, table, cots, rot, rad, src, valid, weights, edges)
    slot_grad = summed[:, atoms:].astype(BF)
    returned = jnp.concatenate(
        [shifted(slot_grad[:, i * halo : (i + 1) * halo], -peer_steps[i]) for i in range(4)], axis=1
    )
    added = jnp.einsum("sa,nsc->nac", send_hot, returned, preferred_element_type=F32)
    total = cots.astype(F32) + summed[:, :atoms] + added
    grad_nodes = total.astype(BF).transpose(1, 0, 2)
    return (grad_nodes, grad_radial, *grads)


def solution(mesh):
    both = ("groups", "graph")
    return jax.shard_map(
        body,
        mesh=mesh,
        in_specs=(
            P(both, None, None), P(both, None, None), P(None, both), P(both, None),
            P(both), P(both), P(both, None), P(), P(), P(),
        ),
        out_specs=(P(both, None, None), P(both, None), P(both), P(both), P(both)),
        check_vma=False,
    )
```

```python
import functools

import jax
import jax.numpy as jnp
from jax import lax
from jax.experimental import pallas as pl
from jax.experimental.pallas import tpu as pltpu
from jax.sharding import PartitionSpec as P

BF = jnp.bfloat16
F32 = jnp.float32
peer_steps = (-2, -1, 1, 2)
order_first = (0, 6, 12, 17, 22)
CB = 32
VMEM_LIMIT = 58 * 2**20


def degrees():
    entry = 0
    for degree in range(7):
        held = min(2 * degree + 1, 5)
        yield degree, held, entry
        entry += held * (2 * degree + 1)


def shifted(block, distance):
    devices = range(lax.axis_size("graph"))
    route = [(i - distance, i) for i in devices if i - distance in devices]
    return lax.ppermute(block, "graph", route)


def dot(left, right):
    return jnp.dot(left, right, preferred_element_type=F32)


def dot_nt(left, right):
    return lax.dot_general(left, right, (((1,), (1,)), ((), ())), preferred_element_type=F32)


def dot_tn(left, right):
    return lax.dot_general(left, right, (((0,), (0,)), ((), ())), preferred_element_type=F32)


def rows(first, count):
    return pl.ds(pl.multiple_of(first, CB), count)


def forward_kernel(
    neigh, ch, widths,
    tab_ref, cot_ref, rot_ref, rad_ref, src_ref, valid_ref,
    gz_ref, g1_ref, g2_ref, rotated_ref, gout_ref,
    xg, cx, inp, rot32, radt,
):
    coefs, slots, _ = tab_ref.shape
    atoms = cot_ref.shape[1]
    ep = rot_ref.shape[1]
    hot = (lax.broadcasted_iota(jnp.int32, (slots, ep), 0) == src_ref[...]).astype(F32).astype(BF)
    edge = lax.broadcasted_iota(jnp.int32, (atoms, ep), 1)
    first = lax.broadcasted_iota(jnp.int32, (atoms, ep), 0) * neigh
    mine = (edge >= first) & (edge < first + neigh) & (valid_ref[...] != 0)
    rep = mine.astype(F32).astype(BF)
    rot32[...] = rot_ref[...].astype(F32)
    radt[...] = rad_ref[...].astype(F32).T

    def gather(n, _):
        at = pl.ds(pl.multiple_of(n * ch, ch), ch)
        xg[at, :] = dot_tn(tab_ref[n], hot).astype(BF)
        cx[at, :] = dot_tn(cot_ref[n], rep).astype(BF)
        return _

    lax.fori_loop(0, coefs, gather, 0)

    def rotate(step, _):
        eb = step // (ch // CB)
        cb = (step % (ch // CB)) * CB
        lanes = pl.ds(pl.multiple_of(eb * 128, 128), 128)
        rad = radt[rows(cb, CB), lanes]
        for degree, held, entry in degrees():
            acc = [None] * held
            accg = [None] * held
            for j in range(2 * degree + 1):
                at = rows((degree * degree + j) * ch + cb, CB)
                x = xg[at, lanes].astype(F32)
                g = cx[at, lanes].astype(F32)
                for m in range(held):
                    k = entry + m * (2 * degree + 1) + j
                    r = rot32[k : k + 1, lanes]
                    acc[m] = r * x if j == 0 else acc[m] + r * x
                    accg[m] = r * g if j == 0 else accg[m] + r * g
            for m in range(held):
                at = rows((order_first[m] + degree) * ch + cb, CB)
                rotated_ref[at, lanes] = acc[m].astype(BF)
                inp[at, lanes] = (acc[m] * rad).astype(BF)
                gout_ref[at, lanes] = accg[m].astype(BF)
        return _

    lax.fori_loop(0, (ep // 128) * (ch // CB), rotate, 0)

    wz, w1, w2 = widths
    half = wz // 2

    def zero_part(i, _):
        at = rows(i * half, half)
        gz_ref[at, :] = dot_nt(inp[at, :], gout_ref[0:wz, :]).astype(gz_ref.dtype)
        return _

    lax.fori_loop(0, 2, zero_part, 0)
    for width, base, out in ((w1, wz, g1_ref), (w2, wz + 2 * w1, g2_ref)):
        tile = width // 2
        plus = gout_ref.at[base : base + width]
        minus = gout_ref.at[base + width : base + 2 * width]

        def pair_part(i, _, width=width, base=base, out=out, tile=tile, plus=plus, minus=minus):
            p = inp[rows(base + i * tile, tile), :]
            m = inp[rows(base + width + i * tile, tile), :]
            at = rows(i * tile, tile)
            out[at, 0:width] = (dot_nt(p, plus[...]) + dot_nt(m, minus[...])).astype(out.dtype)
            out[at, width : 2 * width] = (dot_nt(p, minus[...]) - dot_nt(m, plus[...])).astype(out.dtype)
            return _

        lax.fori_loop(0, 2, pair_part, 0)


def backward_kernel(
    ch, widths,
    rot_ref, rad_ref, src_ref, gout_ref, rotated_ref, w0_ref, w1_ref, w2_ref,
    sum_ref, grad_ref,
    gin, eg, rot32, radt, grt,
):
    coefs, slots, _ = sum_ref.shape
    ep = rot_ref.shape[1]
    edges = grad_ref.shape[0]
    hot = (lax.broadcasted_iota(jnp.int32, (slots, ep), 0) == src_ref[...]).astype(F32).astype(BF)
    rot32[...] = rot_ref[...].astype(F32)
    radt[...] = rad_ref[...].astype(F32).T
    wz, w1, w2 = widths
    half = wz // 2

    def zero_part(i, _):
        at = rows(i * half, half)
        gin[at, :] = dot(w0_ref[at, :], gout_ref[0:wz, :])
        return _

    lax.fori_loop(0, 2, zero_part, 0)
    for width, base, w_ref in ((w1, wz, w1_ref), (w2, wz + 2 * w1, w2_ref)):
        tile = width // 2
        plus = gout_ref.at[base : base + width]
        minus = gout_ref.at[base + width : base + 2 * width]

        def pair_part(i, _, width=width, base=base, w_ref=w_ref, tile=tile, plus=plus, minus=minus):
            at = rows(i * tile, tile)
            a = w_ref[at, 0:width]
            b = w_ref[at, width : 2 * width]
            gin[rows(base + i * tile, tile), :] = dot(a, plus[...]) + dot(b, minus[...])
            gin[rows(base + width + i * tile, tile), :] = dot(a, minus[...]) - dot(b, plus[...])
            return _

        lax.fori_loop(0, 2, pair_part, 0)

    def rotate(step, _):
        eb = step // (ch // CB)
        cb = (step % (ch // CB)) * CB
        lanes = pl.ds(pl.multiple_of(eb * 128, 128), 128)
        rad = radt[rows(cb, CB), lanes]
        total = jnp.zeros((CB, 128), F32)
        for degree, held, entry in degrees():
            weighted = []
            for m in range(held):
                at = rows((order_first[m] + degree) * ch + cb, CB)
                value = gin[at, lanes]
                total = total + value * rotated_ref[at, lanes].astype(F32)
                weighted.append(value * rad)
            for j in range(2 * degree + 1):
                acc = None
                for m in range(held):
                    k = entry + m * (2 * degree + 1) + j
                    term = rot32[k : k + 1, lanes] * weighted[m]
                    acc = term if m == 0 else acc + term
                eg[rows((degree * degree + j) * ch + cb, CB), lanes] = acc.astype(BF)
        grt[rows(cb, CB), lanes] = total
        return _

    lax.fori_loop(0, (ep // 128) * (ch // CB), rotate, 0)
    grad_ref[...] = grt[...].T[:edges].astype(BF)

    def scatter(i, _):
        part = dot_nt(hot, eg[pl.ds(pl.multiple_of(i * 7 * ch, ch), 7 * ch), :])
        for j in range(7):
            sum_ref[i * 7 + j] = part[:, j * ch : (j + 1) * ch]
        return _

    lax.fori_loop(0, coefs // 7, scatter, 0)


def fused_kernel(
    neigh, ch, widths, graph,
    node_ref, cot_ref, rot_ref, rad_ref, src_ref, valid_ref, sent_ref, back_ref, w0_ref, w1_ref, w2_ref,
    nodes_out, grad_ref, oz_ref, o1_ref, o2_ref,
    xg, cx, inp, gout, rotated, rot32, radt, grt, halo_out, halo_in, slot_out, slot_in, halos, local, *rest,
):
    staged = rest[0:3]
    landed = (rest[3:7], rest[7:11], rest[11:15])
    send_sem, recv_sem, halo_send, halo_recv = rest[15:19]
    outs = (oz_ref, o1_ref, o2_ref)
    me = lax.axis_index("graph")
    bits = [me & 1, (me >> 1) & 1, (me >> 2) & 1, (me >> 3) & 1]
    partners = [me + (1 << b) * (1 - 2 * bits[b]) for b in range(4)]
    coefs, atoms, _ = node_ref.shape
    halo = sent_ref.shape[0] // 4
    slots = atoms + 4 * halo
    halo_in[...] = jnp.zeros_like(halo_in)
    slot_in[...] = jnp.zeros_like(slot_in)
    near = [(me + step, (me + step >= 0) & (me + step < graph)) for step in peer_steps]
    barrier = pltpu.get_barrier_semaphore()
    for other, there in near:

        @pl.when(there)
        def _(other=other):
            pl.semaphore_signal(
                barrier, inc=1, device_id={"graph": other}, device_id_type=pl.DeviceIdType.MESH
            )

    for partner in partners:
        pl.semaphore_signal(barrier, inc=1, device_id={"graph": partner}, device_id_type=pl.DeviceIdType.MESH)

    firsts = [0]
    for stage in range(4):
        firsts.append(firsts[-1] + bits[stage] * (8 >> stage))

    def copy_of(which, stage):
        count = 8 >> stage
        at = firsts[stage] + (1 - bits[stage]) * count
        return pltpu.make_async_remote_copy(
            src_ref=staged[which].at[pl.ds(at, count)],
            dst_ref=landed[which][stage],
            send_sem=send_sem.at[which * 4 + stage],
            recv_sem=recv_sem.at[which * 4 + stage],
            device_id={"graph": partners[stage]},
            device_id_type=pl.DeviceIdType.MESH,
        )

    def advance(which, stage):
        copy_of(which, stage).wait_recv()
        count = 8 >> stage
        if stage == 3:
            outs[which][...] = staged[which][firsts[4]].astype(F32) + landed[which][3][0].astype(F32)
            return
        buffer, part, first = staged[which], landed[which][stage], firsts[stage + 1]

        def add(i, _):
            buffer[first + i] = (buffer[first + i].astype(F32) + part[i].astype(F32)).astype(BF)
            return _

        lax.fori_loop(0, count, add, 0)
        copy_of(which, stage + 1).start()

    def halo_copy(block, back):
        towards = 3 - block if back else block
        return pltpu.make_async_remote_copy(
            src_ref=(slot_out if back else halo_out).at[block],
            dst_ref=(slot_in if back else halo_in).at[block],
            send_sem=halo_send.at[4 * back + block],
            recv_sem=halo_recv.at[4 * back + block],
            device_id={"graph": near[towards][0]},
            device_id_type=pl.DeviceIdType.MESH,
        )

    def halo_each(back, act, incoming):
        for block in range(4):
            side = 3 - block if bool(back) != incoming else block

            @pl.when(near[side][1])
            def _(block=block):
                getattr(halo_copy(block, back), act)()

    def pack(buffer, q, low, high):
        for block in range(4):
            at = slice(block * halo, (block + 1) * halo)
            buffer[block, q] = jnp.concatenate([low[at], high[at]], axis=0).astype(BF)

    def unpack(buffer, q, odd):
        parts = [buffer[block, q].astype(F32)[odd * halo : (odd + 1) * halo] for block in range(4)]
        return jnp.concatenate(parts, axis=0).astype(BF)

    def send_pair(q, _):
        pack(halo_out, q, dot(sent_ref[...], node_ref[2 * q]), dot(sent_ref[...], node_ref[2 * q + 1]))
        return _

    lax.fori_loop(0, coefs // 2, send_pair, 0)
    last = dot(sent_ref[...], node_ref[coefs - 1])
    pack(halo_out, coefs // 2, last, last)
    peers = sum(there.astype(jnp.int32) for _, there in near)
    pl.semaphore_wait(barrier, 4 + peers)
    halo_each(0, "start", False)

    ep = rot_ref.shape[1]
    edges = grad_ref.shape[0]
    wz, w1, w2 = widths
    hot = (lax.broadcasted_iota(jnp.int32, (slots, ep), 0) == src_ref[...]).astype(F32).astype(BF)
    edge = lax.broadcasted_iota(jnp.int32, (atoms, ep), 1)
    first_edge = lax.broadcasted_iota(jnp.int32, (atoms, ep), 0) * neigh
    mine = (edge >= first_edge) & (edge < first_edge + neigh) & (valid_ref[...] != 0)
    rep = mine.astype(F32).astype(BF)
    rot32[...] = rot_ref[...].astype(F32)
    radt[...] = rad_ref[...].astype(F32).T

    def gather_cot(i, _):
        at = pl.ds(pl.multiple_of(i * 7 * ch, ch), 7 * ch)
        wide = jnp.concatenate([cot_ref[i * 7 + j] for j in range(7)], axis=1)
        cx[at, :] = dot_tn(wide, rep).astype(BF)
        return _

    lax.fori_loop(0, coefs // 7, gather_cot, 0)
    halo_each(0, "wait_recv", True)

    def receive_pair(q, _):
        halos[2 * q] = unpack(halo_in, q, 0)
        halos[2 * q + 1] = unpack(halo_in, q, 1)
        return _

    lax.fori_loop(0, coefs // 2, receive_pair, 0)
    halos[coefs - 1] = unpack(halo_in, coefs // 2, 0)

    def gather(i, _):
        at = pl.ds(pl.multiple_of(i * 7 * ch, ch), 7 * ch)
        wide = jnp.concatenate(
            [jnp.concatenate([node_ref[i * 7 + j], halos[i * 7 + j]], axis=0) for j in range(7)], axis=1
        )
        xg[at, :] = dot_tn(wide, hot).astype(BF)
        return _

    lax.fori_loop(0, coefs // 7, gather, 0)

    def rotate(step, _):
        eb = step // (ch // CB)
        cb = (step % (ch // CB)) * CB
        lanes = pl.ds(pl.multiple_of(eb * 128, 128), 128)
        rad = radt[rows(cb, CB), lanes]
        for degree, held, entry in degrees():
            acc = [None] * held
            accg = [None] * held
            for j in range(2 * degree + 1):
                at = rows((degree * degree + j) * ch + cb, CB)
                x = xg[at, lanes].astype(F32)
                g = cx[at, lanes].astype(F32)
                for m in range(held):
                    k = entry + m * (2 * degree + 1) + j
                    r = rot32[k : k + 1, lanes]
                    acc[m] = r * x if j == 0 else acc[m] + r * x
                    accg[m] = r * g if j == 0 else accg[m] + r * g
            for m in range(held):
                at = rows((order_first[m] + degree) * ch + cb, CB)
                rotated[at, lanes] = acc[m].astype(BF)
                inp[at, lanes] = (acc[m] * rad).astype(BF)
                gout[at, lanes] = accg[m].astype(BF)
        return _

    lax.fori_loop(0, (ep // 128) * (ch // CB), rotate, 0)

    def place(which, i, columns, value):
        height = value.shape[0] // 8
        for jj in range(8):
            position = (jj & 1) * 8 + ((jj >> 1) & 1) * 4 + ((jj >> 2) & 1) * 2 + i
            staged[which][position, :, columns] = value[jj * height : (jj + 1) * height].astype(BF)

    def weight_zero():
        half = wz // 2

        def part(i, _):
            place(0, i, slice(0, wz), dot_nt(inp[rows(i * half, half), :], gout[0:wz, :]))
            return _

        lax.fori_loop(0, 2, part, 0)

    def weight_pair(which, width, base):
        tile = width // 2
        plus = gout.at[base : base + width]
        minus = gout.at[base + width : base + 2 * width]

        def part(i, _):
            p = inp[rows(base + i * tile, tile), :]
            m = inp[rows(base + width + i * tile, tile), :]
            place(which, i, slice(0, width), dot_nt(p, plus[...]) + dot_nt(m, minus[...]))
            place(which, i, slice(width, 2 * width), dot_nt(p, minus[...]) - dot_nt(m, plus[...]))
            return _

        lax.fori_loop(0, 2, part, 0)

    gin = cx

    def back_zero():
        half = wz // 2

        def part(i, _):
            at = rows(i * half, half)
            gin[at, :] = dot(w0_ref[at, :], gout[0:wz, :]).astype(BF)
            return _

        lax.fori_loop(0, 2, part, 0)

    def back_pair(width, base, w_ref):
        tile = width // 2
        plus = gout.at[base : base + width]
        minus = gout.at[base + width : base + 2 * width]

        def part(i, _):
            at = rows(i * tile, tile)
            a = w_ref[at, 0:width]
            b = w_ref[at, width : 2 * width]
            gin[rows(base + i * tile, tile), :] = (dot(a, plus[...]) + dot(b, minus[...])).astype(BF)
            gin[rows(base + width + i * tile, tile), :] = (dot(a, minus[...]) - dot(b, plus[...])).astype(BF)
            return _

        lax.fori_loop(0, 2, part, 0)

    weight_pair(1, w1, wz)
    copy_of(1, 0).start()
    weight_pair(2, w2, wz + 2 * w1)
    copy_of(2, 0).start()
    advance(1, 0)
    weight_zero()
    copy_of(0, 0).start()
    advance(2, 0)
    back_zero()
    advance(0, 0)
    back_pair(w1, wz, w1_ref)
    advance(1, 1)
    back_pair(w2, wz + 2 * w1, w2_ref)

    eg = xg

    def rotate_back(step, _):
        eb = step // (ch // CB)
        cb = (step % (ch // CB)) * CB
        lanes = pl.ds(pl.multiple_of(eb * 128, 128), 128)
        rad = radt[rows(cb, CB), lanes]
        total = jnp.zeros((CB, 128), F32)
        for degree, held, entry in degrees():
            weighted = []
            for m in range(held):
                at = rows((order_first[m] + degree) * ch + cb, CB)
                value = gin[at, lanes].astype(F32)
                total = total + value * rotated[at, lanes].astype(F32)
                weighted.append(value * rad)
            for j in range(2 * degree + 1):
                acc = None
                for m in range(held):
                    k = entry + m * (2 * degree + 1) + j
                    term = rot32[k : k + 1, lanes] * weighted[m]
                    acc = term if m == 0 else acc + term
                eg[rows((degree * degree + j) * ch + cb, CB), lanes] = acc.astype(BF)
        grt[rows(cb, CB), lanes] = total
        return _

    steps = (ep // 128) * (ch // CB)
    lax.fori_loop(0, steps // 2, rotate_back, 0)
    advance(2, 1)
    advance(1, 2)
    lax.fori_loop(steps // 2, steps, rotate_back, 0)
    advance(0, 1)
    advance(2, 2)
    grad_ref[...] = grt[...].T[:edges].astype(BF)

    def scatter(q):
        part = dot_nt(hot, eg[pl.ds(pl.multiple_of(q * 2 * ch, ch), 2 * ch), :])
        low, high = part[:, 0:ch], part[:, ch : 2 * ch]
        local[2 * q] = low[:atoms] + cot_ref[2 * q].astype(F32)
        local[2 * q + 1] = high[:atoms] + cot_ref[2 * q + 1].astype(F32)
        pack(slot_out, q, low[atoms:], high[atoms:])

    def scatter_some(i, _):
        for j in range(4):
            scatter(i * 4 + j)
        return _

    lax.fori_loop(0, coefs // 8, scatter_some, 0)
    tail = dot_nt(hot, eg[(coefs - 1) * ch : coefs * ch, :])
    local[coefs - 1] = tail[:atoms] + cot_ref[coefs - 1].astype(F32)
    pack(slot_out, coefs // 2, tail[atoms:], tail[atoms:])
    halo_each(1, "start", False)
    advance(1, 3)
    advance(0, 2)
    advance(2, 3)
    halo_each(1, "wait_recv", True)

    def finish(n, q, odd):
        nodes_out[n] = (local[n] + dot(back_ref[...], unpack(slot_in, q, odd))).astype(BF)

    def finish_pair(q, _):
        finish(2 * q, q, 0)
        finish(2 * q + 1, q, 1)
        return _

    lax.fori_loop(0, coefs // 2, finish_pair, 0)
    finish(coefs - 1, coefs // 2, 0)
    advance(0, 3)
    for which in range(3):
        for stage in range(4):
            copy_of(which, stage).wait_send()
    halo_each(0, "wait_send", False)
    halo_each(1, "wait_send", False)


def fused(neigh, ch, widths, graph, nodes, cots, rot, rad, src, valid, send_hot, weights, edges):
    coefs, atoms, _ = nodes.shape
    halo = send_hot.shape[0] // 4
    packed, ep = rot.shape
    feats = widths[0] + 2 * widths[1] + 2 * widths[2]
    whole = pl.BlockSpec(memory_space=pltpu.VMEM)
    parts = [(w.shape[0] // graph, w.shape[1]) for w in weights]
    scratch = [
        pltpu.VMEM((coefs * ch, ep), BF),
        pltpu.VMEM((coefs * ch, ep), BF),
        pltpu.VMEM((feats, ep), BF),
        pltpu.VMEM((feats, ep), BF),
        pltpu.VMEM((feats, ep), BF),
        pltpu.VMEM((packed, ep), F32),
        pltpu.VMEM((ch, ep), F32),
        pltpu.VMEM((ch, ep), F32),
    ]
    scratch += [pltpu.VMEM((4, coefs // 2 + 1, 2 * halo, ch), BF) for _ in range(4)]
    scratch += [pltpu.VMEM((coefs, 4 * halo, ch), BF), pltpu.VMEM((coefs, atoms, ch), F32)]
    scratch += [pltpu.VMEM((graph, *part), BF) for part in parts]
    scratch += [pltpu.VMEM((8 >> stage, *part), BF) for part in parts for stage in range(4)]
    scratch += [pltpu.SemaphoreType.DMA((count,)) for count in (12, 12, 8, 8)]
    return pl.pallas_call(
        functools.partial(fused_kernel, neigh, ch, widths, graph),
        out_shape=(
            jax.ShapeDtypeStruct((coefs, atoms, ch), BF),
            jax.ShapeDtypeStruct((edges, ch), BF),
            *(jax.ShapeDtypeStruct(part, F32) for part in parts),
        ),
        in_specs=[whole] * 11,
        out_specs=[whole] * 5,
        scratch_shapes=scratch,
        compiler_params=pltpu.CompilerParams(
            vmem_limit_bytes=VMEM_LIMIT, collective_id=0, has_side_effects=True
        ),
        name="fused",
    )(nodes, cots, rot, rad, src, valid, send_hot, send_hot.T, *weights)


def apart(neigh, ch, widths, table, cots, rot, rad, src, valid, weights, edges):
    w_zero, w_one, w_two = weights
    coefs, slots, _ = table.shape
    packed, ep = rot.shape
    feats = widths[0] + 2 * widths[1] + 2 * widths[2]
    params = pltpu.CompilerParams(vmem_limit_bytes=VMEM_LIMIT)
    whole = pl.BlockSpec(memory_space=pltpu.VMEM)
    gz, g1, g2, rotated, gout = pl.pallas_call(
        functools.partial(forward_kernel, neigh, ch, widths),
        out_shape=(
            jax.ShapeDtypeStruct(w_zero.shape, BF),
            jax.ShapeDtypeStruct(w_one.shape, BF),
            jax.ShapeDtypeStruct(w_two.shape, BF),
            jax.ShapeDtypeStruct((feats, ep), BF),
            jax.ShapeDtypeStruct((feats, ep), BF),
        ),
        in_specs=[whole] * 6,
        out_specs=[whole] * 5,
        scratch_shapes=[
            pltpu.VMEM((coefs * ch, ep), BF),
            pltpu.VMEM((coefs * ch, ep), BF),
            pltpu.VMEM((feats, ep), BF),
            pltpu.VMEM((packed, ep), F32),
            pltpu.VMEM((ch, ep), F32),
        ],
        compiler_params=params,
        name="forward",
    )(table, cots, rot, rad, src, valid)
    grads = [
        lax.psum_scatter(g.reshape(-1), "graph", scatter_dimension=0, tiled=True).astype(F32)
        for g in (gz, g1, g2)
    ]
    summed, grad_radial = pl.pallas_call(
        functools.partial(backward_kernel, ch, widths),
        out_shape=(
            jax.ShapeDtypeStruct((coefs, slots, ch), F32),
            jax.ShapeDtypeStruct((edges, ch), BF),
        ),
        in_specs=[whole] * 8,
        out_specs=[whole] * 2,
        scratch_shapes=[
            pltpu.VMEM((feats, ep), F32),
            pltpu.VMEM((coefs * ch, ep), BF),
            pltpu.VMEM((packed, ep), F32),
            pltpu.VMEM((ch, ep), F32),
            pltpu.VMEM((ch, ep), F32),
        ],
        compiler_params=params,
        cost_estimate=pl.CostEstimate(flops=8_000_000_000, bytes_accessed=20_000_000, transcendentals=0),
        name="backward",
    )(rot, rad, src, gout, rotated, w_zero, w_one, w_two)
    return (summed, grad_radial, *grads)


def body(node_irreps, cotangent, rotation, radial, edge_source, edge_valid, send_rows, w_zero, w_one, w_two):
    atoms, coefs, ch = node_irreps.shape
    halo = send_rows.shape[1]
    edges = edge_source.shape[0]
    neigh = edges // atoms
    ep = -(-edges // 128) * 128
    pad = ep - edges
    widths = (w_zero.shape[0], w_one.shape[0], w_two.shape[0])
    feats = widths[0] + 2 * widths[1] + 2 * widths[2]
    send_hot = (send_rows.reshape(-1)[:, None] == jnp.arange(atoms, dtype=jnp.int32)[None, :]).astype(BF)
    nodes = node_irreps.transpose(1, 0, 2)
    cots = cotangent.transpose(1, 0, 2)
    rot = jnp.pad(rotation, ((0, 0), (0, pad)))
    rad = jnp.pad(radial, ((0, pad), (0, 0)))
    src = jnp.pad(edge_source, (0, pad), constant_values=-1)[None, :]
    valid = jnp.pad(edge_valid, (0, pad))[None, :]
    weights = (w_zero, w_one, w_two)
    graph = lax.axis_size("graph")
    if graph == 16 and halo == 8 and coefs == 49 and all(w.shape[0] % (8 * graph) == 0 for w in weights):
        total, grad_radial, *grads = fused(
            neigh, ch, widths, graph, nodes, cots, rot, rad, src, valid, send_hot, weights, edges
        )
        grads = [g.reshape(-1) for g in grads]
    else:
        outgoing = jnp.einsum("sa,nac->nsc", send_hot, nodes, preferred_element_type=F32).astype(BF)
        incoming = [shifted(outgoing[:, i * halo : (i + 1) * halo], peer_steps[i]) for i in range(4)]
        table = jnp.concatenate([nodes, *incoming], axis=1)
        summed, grad_radial, *grads = apart(neigh, ch, widths, table, cots, rot, rad, src, valid, weights, edges)
        slot_grad = summed[:, atoms:].astype(BF)
        returned = jnp.concatenate(
            [shifted(slot_grad[:, i * halo : (i + 1) * halo], -peer_steps[i]) for i in range(4)], axis=1
        )
        added = jnp.einsum("sa,nsc->nac", send_hot, returned, preferred_element_type=F32)
        total = cots.astype(F32) + summed[:, :atoms] + added
        total = total.astype(BF)
    return (total.transpose(1, 0, 2), grad_radial, *grads)


def solution(mesh):
    both = ("groups", "graph")
    return jax.shard_map(
        body,
        mesh=mesh,
        in_specs=(
            P(both, None, None), P(both, None, None), P(None, both), P(both, None),
            P(both), P(both), P(both, None), P(), P(), P(),
        ),
        out_specs=(P(both, None, None), P(both, None), P(both), P(both), P(both)),
        check_vma=False,
    )
```

```python
import functools

import jax
import jax.numpy as jnp
from jax import lax
from jax.experimental import pallas as pl
from jax.experimental.pallas import tpu as pltpu
from jax.sharding import PartitionSpec as P

BF = jnp.bfloat16
F32 = jnp.float32
peer_steps = (-2, -1, 1, 2)
order_first = (0, 6, 12, 17, 22)
CB = 32
stage_bits = ((0, 2, 3, 1), (0, 1, 2, 3), (0, 1, 2, 3))
VMEM_LIMIT = 58 * 2**20


def degrees():
    entry = 0
    for degree in range(7):
        held = min(2 * degree + 1, 5)
        yield degree, held, entry
        entry += held * (2 * degree + 1)


def shifted(block, distance):
    devices = range(lax.axis_size("graph"))
    route = [(i - distance, i) for i in devices if i - distance in devices]
    return lax.ppermute(block, "graph", route)


def dot(left, right):
    return jnp.dot(left, right, preferred_element_type=F32)


def dot_nt(left, right):
    return lax.dot_general(left, right, (((1,), (1,)), ((), ())), preferred_element_type=F32)


def dot_tn(left, right):
    return lax.dot_general(left, right, (((0,), (0,)), ((), ())), preferred_element_type=F32)


def rows(first, count):
    return pl.ds(pl.multiple_of(first, CB), count)


def forward_kernel(
    neigh, ch, widths,
    tab_ref, cot_ref, rot_ref, rad_ref, src_ref, valid_ref,
    gz_ref, g1_ref, g2_ref, rotated_ref, gout_ref,
    xg, cx, inp, rot32, radt,
):
    coefs, slots, _ = tab_ref.shape
    atoms = cot_ref.shape[1]
    ep = rot_ref.shape[1]
    hot = (lax.broadcasted_iota(jnp.int32, (slots, ep), 0) == src_ref[...]).astype(F32).astype(BF)
    edge = lax.broadcasted_iota(jnp.int32, (atoms, ep), 1)
    first = lax.broadcasted_iota(jnp.int32, (atoms, ep), 0) * neigh
    mine = (edge >= first) & (edge < first + neigh) & (valid_ref[...] != 0)
    rep = mine.astype(F32).astype(BF)
    rot32[...] = rot_ref[...].astype(F32)
    radt[...] = rad_ref[...].astype(F32).T

    def gather(n, _):
        at = pl.ds(pl.multiple_of(n * ch, ch), ch)
        xg[at, :] = dot_tn(tab_ref[n], hot).astype(BF)
        cx[at, :] = dot_tn(cot_ref[n], rep).astype(BF)
        return _

    lax.fori_loop(0, coefs, gather, 0)

    def rotate(step, _):
        eb = step // (ch // CB)
        cb = (step % (ch // CB)) * CB
        lanes = pl.ds(pl.multiple_of(eb * 128, 128), 128)
        rad = radt[rows(cb, CB), lanes]
        for degree, held, entry in degrees():
            acc = [None] * held
            accg = [None] * held
            for j in range(2 * degree + 1):
                at = rows((degree * degree + j) * ch + cb, CB)
                x = xg[at, lanes].astype(F32)
                g = cx[at, lanes].astype(F32)
                for m in range(held):
                    k = entry + m * (2 * degree + 1) + j
                    r = rot32[k : k + 1, lanes]
                    acc[m] = r * x if j == 0 else acc[m] + r * x
                    accg[m] = r * g if j == 0 else accg[m] + r * g
            for m in range(held):
                at = rows((order_first[m] + degree) * ch + cb, CB)
                rotated_ref[at, lanes] = acc[m].astype(BF)
                inp[at, lanes] = (acc[m] * rad).astype(BF)
                gout_ref[at, lanes] = accg[m].astype(BF)
        return _

    lax.fori_loop(0, (ep // 128) * (ch // CB), rotate, 0)

    wz, w1, w2 = widths
    half = wz // 2

    def zero_part(i, _):
        at = rows(i * half, half)
        gz_ref[at, :] = dot_nt(inp[at, :], gout_ref[0:wz, :]).astype(gz_ref.dtype)
        return _

    lax.fori_loop(0, 2, zero_part, 0)
    for width, base, out in ((w1, wz, g1_ref), (w2, wz + 2 * w1, g2_ref)):
        tile = width // 2
        plus = gout_ref.at[base : base + width]
        minus = gout_ref.at[base + width : base + 2 * width]

        def pair_part(i, _, width=width, base=base, out=out, tile=tile, plus=plus, minus=minus):
            p = inp[rows(base + i * tile, tile), :]
            m = inp[rows(base + width + i * tile, tile), :]
            at = rows(i * tile, tile)
            out[at, 0:width] = (dot_nt(p, plus[...]) + dot_nt(m, minus[...])).astype(out.dtype)
            out[at, width : 2 * width] = (dot_nt(p, minus[...]) - dot_nt(m, plus[...])).astype(out.dtype)
            return _

        lax.fori_loop(0, 2, pair_part, 0)


def backward_kernel(
    ch, widths,
    rot_ref, rad_ref, src_ref, gout_ref, rotated_ref, w0_ref, w1_ref, w2_ref,
    sum_ref, grad_ref,
    gin, eg, rot32, radt, grt,
):
    coefs, slots, _ = sum_ref.shape
    ep = rot_ref.shape[1]
    edges = grad_ref.shape[0]
    hot = (lax.broadcasted_iota(jnp.int32, (slots, ep), 0) == src_ref[...]).astype(F32).astype(BF)
    rot32[...] = rot_ref[...].astype(F32)
    radt[...] = rad_ref[...].astype(F32).T
    wz, w1, w2 = widths
    half = wz // 2

    def zero_part(i, _):
        at = rows(i * half, half)
        gin[at, :] = dot(w0_ref[at, :], gout_ref[0:wz, :])
        return _

    lax.fori_loop(0, 2, zero_part, 0)
    for width, base, w_ref in ((w1, wz, w1_ref), (w2, wz + 2 * w1, w2_ref)):
        tile = width // 2
        plus = gout_ref.at[base : base + width]
        minus = gout_ref.at[base + width : base + 2 * width]

        def pair_part(i, _, width=width, base=base, w_ref=w_ref, tile=tile, plus=plus, minus=minus):
            at = rows(i * tile, tile)
            a = w_ref[at, 0:width]
            b = w_ref[at, width : 2 * width]
            gin[rows(base + i * tile, tile), :] = dot(a, plus[...]) + dot(b, minus[...])
            gin[rows(base + width + i * tile, tile), :] = dot(a, minus[...]) - dot(b, plus[...])
            return _

        lax.fori_loop(0, 2, pair_part, 0)

    def rotate(step, _):
        eb = step // (ch // CB)
        cb = (step % (ch // CB)) * CB
        lanes = pl.ds(pl.multiple_of(eb * 128, 128), 128)
        rad = radt[rows(cb, CB), lanes]
        total = jnp.zeros((CB, 128), F32)
        for degree, held, entry in degrees():
            weighted = []
            for m in range(held):
                at = rows((order_first[m] + degree) * ch + cb, CB)
                value = gin[at, lanes]
                total = total + value * rotated_ref[at, lanes].astype(F32)
                weighted.append(value * rad)
            for j in range(2 * degree + 1):
                acc = None
                for m in range(held):
                    k = entry + m * (2 * degree + 1) + j
                    term = rot32[k : k + 1, lanes] * weighted[m]
                    acc = term if m == 0 else acc + term
                eg[rows((degree * degree + j) * ch + cb, CB), lanes] = acc.astype(BF)
        grt[rows(cb, CB), lanes] = total
        return _

    lax.fori_loop(0, (ep // 128) * (ch // CB), rotate, 0)
    grad_ref[...] = grt[...].T[:edges].astype(BF)

    def scatter(i, _):
        part = dot_nt(hot, eg[pl.ds(pl.multiple_of(i * 7 * ch, ch), 7 * ch), :])
        for j in range(7):
            sum_ref[i * 7 + j] = part[:, j * ch : (j + 1) * ch]
        return _

    lax.fori_loop(0, coefs // 7, scatter, 0)


def fused_kernel(
    neigh, ch, widths, graph,
    node_ref, cot_ref, rot_ref, rad_ref, src_ref, valid_ref, sent_ref, back_ref, w0_ref, w1_ref, w2_ref,
    nodes_out, grad_ref, oz_ref, o1_ref, o2_ref,
    xg, cx, inp, gout, rotated, rot32, radt, grt, src_wide, valid_wide, halo_out, halo_in, slot_out, slot_in, halos, local, *rest,
):
    staged = rest[0:3]
    landed = (rest[3:7], rest[7:11], rest[11:15])
    send_sem, recv_sem, halo_send, halo_recv = rest[15:19]
    outs = (oz_ref, o1_ref, o2_ref)
    me = lax.axis_index("graph")
    bits = [me & 1, (me >> 1) & 1, (me >> 2) & 1, (me >> 3) & 1]
    partners = [me + (1 << b) * (1 - 2 * bits[b]) for b in range(4)]
    coefs, atoms, _ = node_ref.shape
    halo = sent_ref.shape[0] // 4
    slots = atoms + 4 * halo
    halo_in[...] = jnp.zeros_like(halo_in)
    slot_in[...] = jnp.zeros_like(slot_in)
    near = [(me + step, (me + step >= 0) & (me + step < graph)) for step in peer_steps]
    barrier = pltpu.get_barrier_semaphore()
    for other, there in near:

        @pl.when(there)
        def _(other=other):
            pl.semaphore_signal(
                barrier, inc=1, device_id={"graph": other}, device_id_type=pl.DeviceIdType.MESH
            )

    for partner in partners:
        pl.semaphore_signal(barrier, inc=1, device_id={"graph": partner}, device_id_type=pl.DeviceIdType.MESH)

    firsts = []
    for order in stage_bits:
        first = [0]
        for stage in range(4):
            first.append(first[-1] + bits[order[stage]] * (8 >> stage))
        firsts.append(first)

    def copy_of(which, stage):
        count = 8 >> stage
        bit = stage_bits[which][stage]
        at = firsts[which][stage] + (1 - bits[bit]) * count
        return pltpu.make_async_remote_copy(
            src_ref=staged[which].at[pl.ds(at, count)],
            dst_ref=landed[which][stage],
            send_sem=send_sem.at[which * 4 + stage],
            recv_sem=recv_sem.at[which * 4 + stage],
            device_id={"graph": partners[bit]},
            device_id_type=pl.DeviceIdType.MESH,
        )

    def advance(which, stage):
        copy_of(which, stage).wait_recv()
        count = 8 >> stage
        if stage == 3:
            total = staged[which][firsts[which][4]].astype(F32) + landed[which][3][0].astype(F32)
            blocks = total.shape[1] // 128
            for block in range(blocks):
                outs[which][pl.ds(block, total.shape[0], stride=blocks), :] = total[
                    :, block * 128 : (block + 1) * 128
                ]
            return
        buffer, part, first = staged[which], landed[which][stage], firsts[which][stage + 1]

        def add(i, _):
            buffer[first + i] = (buffer[first + i].astype(F32) + part[i].astype(F32)).astype(BF)
            return _

        lax.fori_loop(0, count, add, 0)
        copy_of(which, stage + 1).start()

    def halo_copy(block, back):
        towards = 3 - block if back else block
        return pltpu.make_async_remote_copy(
            src_ref=(slot_out if back else halo_out).at[block],
            dst_ref=(slot_in if back else halo_in).at[block],
            send_sem=halo_send.at[4 * back + block],
            recv_sem=halo_recv.at[4 * back + block],
            device_id={"graph": near[towards][0]},
            device_id_type=pl.DeviceIdType.MESH,
        )

    def halo_each(back, act, incoming):
        for block in range(4):
            side = 3 - block if bool(back) != incoming else block

            @pl.when(near[side][1])
            def _(block=block):
                getattr(halo_copy(block, back), act)()

    def pack(buffer, q, low, high):
        for block in range(4):
            at = slice(block * halo, (block + 1) * halo)
            buffer[block, q] = jnp.concatenate([low[at], high[at]], axis=0).astype(BF)

    def unpack(buffer, q, odd):
        parts = [buffer[block, q].astype(F32)[odd * halo : (odd + 1) * halo] for block in range(4)]
        return jnp.concatenate(parts, axis=0).astype(BF)

    def send_pair(q, _):
        pack(halo_out, q, dot(sent_ref[...], node_ref[2 * q]), dot(sent_ref[...], node_ref[2 * q + 1]))
        return _

    lax.fori_loop(0, coefs // 2, send_pair, 0)
    last = dot(sent_ref[...], node_ref[coefs - 1])
    pack(halo_out, coefs // 2, last, last)
    peers = sum(there.astype(jnp.int32) for _, there in near)
    pl.semaphore_wait(barrier, 4 + peers)
    halo_each(0, "start", False)

    ep = rot32.shape[1]
    edges = grad_ref.shape[0]
    src_wide[...] = jnp.full_like(src_wide, -1)
    valid_wide[...] = jnp.zeros_like(valid_wide)
    src_wide[:, :edges] = src_ref[...]
    valid_wide[:, :edges] = valid_ref[...]
    wz, w1, w2 = widths
    hot = (lax.broadcasted_iota(jnp.int32, (slots, ep), 0) == src_wide[...]).astype(F32).astype(BF)
    edge = lax.broadcasted_iota(jnp.int32, (atoms, ep), 1)
    first_edge = lax.broadcasted_iota(jnp.int32, (atoms, ep), 0) * neigh
    mine = (edge >= first_edge) & (edge < first_edge + neigh) & (valid_wide[...] != 0)
    rep = mine.astype(F32).astype(BF)
    rot32[:, (edges // 128) * 128 :] = jnp.zeros_like(rot32[:, (edges // 128) * 128 :])
    rot32[:, :edges] = rot_ref[...].astype(F32)
    for low in range(0, ep, 128):
        block = rad_ref[low : min(low + 128, edges), :].astype(F32)
        if block.shape[0] < 128:
            block = jnp.concatenate([block, jnp.zeros((128 - block.shape[0], ch), F32)], axis=0)
        radt[:, low : low + 128] = block.T

    def gather_cot(i, _):
        at = pl.ds(pl.multiple_of(i * 7 * ch, ch), 7 * ch)
        wide = jnp.concatenate([cot_ref[i * 7 + j] for j in range(7)], axis=1)
        cx[at, :] = dot_tn(wide, rep).astype(BF)
        return _

    lax.fori_loop(0, coefs // 7, gather_cot, 0)
    halo_each(0, "wait_recv", True)

    def receive_pair(q, _):
        halos[2 * q] = unpack(halo_in, q, 0)
        halos[2 * q + 1] = unpack(halo_in, q, 1)
        return _

    lax.fori_loop(0, coefs // 2, receive_pair, 0)
    halos[coefs - 1] = unpack(halo_in, coefs // 2, 0)

    def gather(i, _):
        at = pl.ds(pl.multiple_of(i * 7 * ch, ch), 7 * ch)
        wide = jnp.concatenate(
            [jnp.concatenate([node_ref[i * 7 + j], halos[i * 7 + j]], axis=0) for j in range(7)], axis=1
        )
        xg[at, :] = dot_tn(wide, hot).astype(BF)
        return _

    lax.fori_loop(0, coefs // 7, gather, 0)

    def rotate(step, _):
        eb = step // (ch // CB)
        cb = (step % (ch // CB)) * CB
        lanes = pl.ds(pl.multiple_of(eb * 128, 128), 128)
        rad = radt[rows(cb, CB), lanes]
        for degree, held, entry in degrees():
            acc = [None] * held
            accg = [None] * held
            for j in range(2 * degree + 1):
                at = rows((degree * degree + j) * ch + cb, CB)
                x = xg[at, lanes].astype(F32)
                g = cx[at, lanes].astype(F32)
                for m in range(held):
                    k = entry + m * (2 * degree + 1) + j
                    r = rot32[k : k + 1, lanes]
                    acc[m] = r * x if j == 0 else acc[m] + r * x
                    accg[m] = r * g if j == 0 else accg[m] + r * g
            for m in range(held):
                at = rows((order_first[m] + degree) * ch + cb, CB)
                rotated[at, lanes] = acc[m].astype(BF)
                inp[at, lanes] = (acc[m] * rad).astype(BF)
                gout[at, lanes] = accg[m].astype(BF)
        return _

    lax.fori_loop(0, (ep // 128) * (ch // CB), rotate, 0)

    def place(which, i, columns, value):
        height = value.shape[0] // 8
        for jj in range(8):
            owner = [jj & 1, (jj >> 1) & 1, (jj >> 2) & 1, i]
            position = sum(owner[bit] * (8 >> stage) for stage, bit in enumerate(stage_bits[which]))
            staged[which][position, :, columns] = value[jj * height : (jj + 1) * height].astype(BF)

    def weight_zero():
        half = wz // 2

        def part(i, _):
            place(0, i, slice(0, wz), dot_nt(inp[rows(i * half, half), :], gout[0:wz, :]))
            return _

        lax.fori_loop(0, 2, part, 0)

    def weight_pair(which, width, base):
        tile = width // 2
        plus = gout.at[base : base + width]
        minus = gout.at[base + width : base + 2 * width]

        def part(i, _):
            p = inp[rows(base + i * tile, tile), :]
            m = inp[rows(base + width + i * tile, tile), :]
            place(which, i, slice(0, width), dot_nt(p, plus[...]) + dot_nt(m, minus[...]))
            place(which, i, slice(width, 2 * width), dot_nt(p, minus[...]) - dot_nt(m, plus[...]))
            return _

        lax.fori_loop(0, 2, part, 0)

    gin = cx

    def back_zero():
        half = wz // 2

        def part(i, _):
            at = rows(i * half, half)
            gin[at, :] = dot(w0_ref[at, :], gout[0:wz, :]).astype(BF)
            return _

        lax.fori_loop(0, 2, part, 0)

    def back_pair(width, base, w_ref):
        tile = width // 2
        plus = gout.at[base : base + width]
        minus = gout.at[base + width : base + 2 * width]

        def part(i, _):
            at = rows(i * tile, tile)
            a = w_ref[at, 0:width]
            b = w_ref[at, width : 2 * width]
            gin[rows(base + i * tile, tile), :] = (dot(a, plus[...]) + dot(b, minus[...])).astype(BF)
            gin[rows(base + width + i * tile, tile), :] = (dot(a, minus[...]) - dot(b, plus[...])).astype(BF)
            return _

        lax.fori_loop(0, 2, part, 0)

    weight_pair(1, w1, wz)
    copy_of(1, 0).start()
    weight_pair(2, w2, wz + 2 * w1)
    copy_of(2, 0).start()
    advance(1, 0)
    weight_zero()
    copy_of(0, 0).start()
    advance(2, 0)
    back_zero()
    advance(0, 0)
    back_pair(w1, wz, w1_ref)
    back_pair(w2, wz + 2 * w1, w2_ref)
    advance(0, 1)

    eg = xg

    def rotate_back(step, _):
        eb = step // (ch // CB)
        cb = (step % (ch // CB)) * CB
        lanes = pl.ds(pl.multiple_of(eb * 128, 128), 128)
        rad = radt[rows(cb, CB), lanes]
        total = jnp.zeros((CB, 128), F32)
        for degree, held, entry in degrees():
            weighted = []
            for m in range(held):
                at = rows((order_first[m] + degree) * ch + cb, CB)
                value = gin[at, lanes].astype(F32)
                total = total + value * rotated[at, lanes].astype(F32)
                weighted.append(value * rad)
            for j in range(2 * degree + 1):
                acc = None
                for m in range(held):
                    k = entry + m * (2 * degree + 1) + j
                    term = rot32[k : k + 1, lanes] * weighted[m]
                    acc = term if m == 0 else acc + term
                eg[rows((degree * degree + j) * ch + cb, CB), lanes] = acc.astype(BF)
        grt[rows(cb, CB), lanes] = total
        return _

    steps = (ep // 128) * (ch // CB)
    lax.fori_loop(0, steps // 4, rotate_back, 0)
    advance(1, 1)
    lax.fori_loop(steps // 4, steps // 2, rotate_back, 0)
    advance(0, 2)
    advance(2, 1)
    lax.fori_loop(steps // 2, 3 * steps // 4, rotate_back, 0)
    advance(1, 2)
    lax.fori_loop(3 * steps // 4, steps, rotate_back, 0)
    grad_ref[...] = grt[...].T[:edges].astype(BF)

    def scatter(q):
        part = dot_nt(hot, eg[pl.ds(pl.multiple_of(q * 2 * ch, ch), 2 * ch), :])
        low, high = part[:, 0:ch], part[:, ch : 2 * ch]
        local[2 * q] = low[:atoms] + cot_ref[2 * q].astype(F32)
        local[2 * q + 1] = high[:atoms] + cot_ref[2 * q + 1].astype(F32)
        pack(slot_out, q, low[atoms:], high[atoms:])

    def scatter_some(i, _):
        for j in range(4):
            scatter(i * 4 + j)
        return _

    lax.fori_loop(0, coefs // 8, scatter_some, 0)
    tail = dot_nt(hot, eg[(coefs - 1) * ch : coefs * ch, :])
    local[coefs - 1] = tail[:atoms] + cot_ref[coefs - 1].astype(F32)
    pack(slot_out, coefs // 2, tail[atoms:], tail[atoms:])
    halo_each(1, "start", False)
    advance(2, 2)
    advance(0, 3)
    advance(1, 3)
    halo_each(1, "wait_recv", True)

    def finish(n, q, odd):
        nodes_out[n] = (local[n] + dot(back_ref[...], unpack(slot_in, q, odd))).astype(BF)

    def finish_pair(q, _):
        finish(2 * q, q, 0)
        finish(2 * q + 1, q, 1)
        return _

    lax.fori_loop(0, coefs // 2, finish_pair, 0)
    finish(coefs - 1, coefs // 2, 0)
    advance(2, 3)
    for which in range(3):
        for stage in range(4):
            copy_of(which, stage).wait_send()
    halo_each(0, "wait_send", False)
    halo_each(1, "wait_send", False)


def fused(neigh, ch, widths, graph, nodes, cots, rot, rad, src, valid, send_hot, weights, edges):
    coefs, atoms, _ = nodes.shape
    halo = send_hot.shape[0] // 4
    packed = rot.shape[0]
    ep = -(-edges // 128) * 128
    feats = widths[0] + 2 * widths[1] + 2 * widths[2]
    whole = pl.BlockSpec(memory_space=pltpu.VMEM)
    parts = [(w.shape[0] // graph, w.shape[1]) for w in weights]
    scratch = [
        pltpu.VMEM((coefs * ch, ep), BF),
        pltpu.VMEM((coefs * ch, ep), BF),
        pltpu.VMEM((feats, ep), BF),
        pltpu.VMEM((feats, ep), BF),
        pltpu.VMEM((feats, ep), BF),
        pltpu.VMEM((packed, ep), F32),
        pltpu.VMEM((ch, ep), F32),
        pltpu.VMEM((ch, ep), F32),
    ]
    scratch += [pltpu.VMEM((1, ep), jnp.int32), pltpu.VMEM((1, ep), jnp.int32)]
    scratch += [pltpu.VMEM((4, coefs // 2 + 1, 2 * halo, ch), BF) for _ in range(4)]
    scratch += [pltpu.VMEM((coefs, 4 * halo, ch), BF), pltpu.VMEM((coefs, atoms, ch), F32)]
    scratch += [pltpu.VMEM((graph, *part), BF) for part in parts]
    scratch += [pltpu.VMEM((8 >> stage, *part), BF) for part in parts for stage in range(4)]
    scratch += [pltpu.SemaphoreType.DMA((count,)) for count in (12, 12, 8, 8)]
    return pl.pallas_call(
        functools.partial(fused_kernel, neigh, ch, widths, graph),
        out_shape=(
            jax.ShapeDtypeStruct((coefs, atoms, ch), BF),
            jax.ShapeDtypeStruct((edges, ch), BF),
            *(jax.ShapeDtypeStruct((part[0] * part[1] // 128, 128), F32) for part in parts),
        ),
        in_specs=[whole] * 11,
        out_specs=[whole] * 5,
        scratch_shapes=scratch,
        compiler_params=pltpu.CompilerParams(
            vmem_limit_bytes=VMEM_LIMIT, collective_id=0, has_side_effects=True
        ),
        name="fused",
    )(nodes, cots, rot, rad, src, valid, send_hot, send_hot.T, *weights)


def apart(neigh, ch, widths, table, cots, rot, rad, src, valid, weights, edges):
    w_zero, w_one, w_two = weights
    coefs, slots, _ = table.shape
    packed, ep = rot.shape
    feats = widths[0] + 2 * widths[1] + 2 * widths[2]
    params = pltpu.CompilerParams(vmem_limit_bytes=VMEM_LIMIT)
    whole = pl.BlockSpec(memory_space=pltpu.VMEM)
    gz, g1, g2, rotated, gout = pl.pallas_call(
        functools.partial(forward_kernel, neigh, ch, widths),
        out_shape=(
            jax.ShapeDtypeStruct(w_zero.shape, BF),
            jax.ShapeDtypeStruct(w_one.shape, BF),
            jax.ShapeDtypeStruct(w_two.shape, BF),
            jax.ShapeDtypeStruct((feats, ep), BF),
            jax.ShapeDtypeStruct((feats, ep), BF),
        ),
        in_specs=[whole] * 6,
        out_specs=[whole] * 5,
        scratch_shapes=[
            pltpu.VMEM((coefs * ch, ep), BF),
            pltpu.VMEM((coefs * ch, ep), BF),
            pltpu.VMEM((feats, ep), BF),
            pltpu.VMEM((packed, ep), F32),
            pltpu.VMEM((ch, ep), F32),
        ],
        compiler_params=params,
        name="forward",
    )(table, cots, rot, rad, src, valid)
    grads = [
        lax.psum_scatter(g.reshape(-1), "graph", scatter_dimension=0, tiled=True).astype(F32)
        for g in (gz, g1, g2)
    ]
    summed, grad_radial = pl.pallas_call(
        functools.partial(backward_kernel, ch, widths),
        out_shape=(
            jax.ShapeDtypeStruct((coefs, slots, ch), F32),
            jax.ShapeDtypeStruct((edges, ch), BF),
        ),
        in_specs=[whole] * 8,
        out_specs=[whole] * 2,
        scratch_shapes=[
            pltpu.VMEM((feats, ep), F32),
            pltpu.VMEM((coefs * ch, ep), BF),
            pltpu.VMEM((packed, ep), F32),
            pltpu.VMEM((ch, ep), F32),
            pltpu.VMEM((ch, ep), F32),
        ],
        compiler_params=params,
        cost_estimate=pl.CostEstimate(flops=8_000_000_000, bytes_accessed=20_000_000, transcendentals=0),
        name="backward",
    )(rot, rad, src, gout, rotated, w_zero, w_one, w_two)
    return (summed, grad_radial, *grads)


def body(node_irreps, cotangent, rotation, radial, edge_source, edge_valid, send_rows, w_zero, w_one, w_two):
    atoms, coefs, ch = node_irreps.shape
    halo = send_rows.shape[1]
    edges = edge_source.shape[0]
    neigh = edges // atoms
    ep = -(-edges // 128) * 128
    pad = ep - edges
    widths = (w_zero.shape[0], w_one.shape[0], w_two.shape[0])
    feats = widths[0] + 2 * widths[1] + 2 * widths[2]
    send_hot = (send_rows.reshape(-1)[:, None] == jnp.arange(atoms, dtype=jnp.int32)[None, :]).astype(BF)
    nodes = node_irreps.transpose(1, 0, 2)
    cots = cotangent.transpose(1, 0, 2)
    weights = (w_zero, w_one, w_two)
    graph = lax.axis_size("graph")
    if graph == 16 and halo == 8 and coefs == 49 and all(w.shape[0] % (8 * graph) == 0 for w in weights):
        total, grad_radial, *grads = fused(
            neigh, ch, widths, graph, nodes, cots, rotation, radial, edge_source[None, :], edge_valid[None, :], send_hot, weights, edges
        )
        grads = [g.reshape(-1) for g in grads]
    else:
        rot = jnp.pad(rotation, ((0, 0), (0, pad)))
        rad = jnp.pad(radial, ((0, pad), (0, 0)))
        src = jnp.pad(edge_source, (0, pad), constant_values=-1)[None, :]
        valid = jnp.pad(edge_valid, (0, pad))[None, :]
        outgoing = jnp.einsum("sa,nac->nsc", send_hot, nodes, preferred_element_type=F32).astype(BF)
        incoming = [shifted(outgoing[:, i * halo : (i + 1) * halo], peer_steps[i]) for i in range(4)]
        table = jnp.concatenate([nodes, *incoming], axis=1)
        summed, grad_radial, *grads = apart(neigh, ch, widths, table, cots, rot, rad, src, valid, weights, edges)
        slot_grad = summed[:, atoms:].astype(BF)
        returned = jnp.concatenate(
            [shifted(slot_grad[:, i * halo : (i + 1) * halo], -peer_steps[i]) for i in range(4)], axis=1
        )
        added = jnp.einsum("sa,nsc->nac", send_hot, returned, preferred_element_type=F32)
        total = cots.astype(F32) + summed[:, :atoms] + added
        total = total.astype(BF)
    return (total.transpose(1, 0, 2), grad_radial, *grads)


def solution(mesh):
    both = ("groups", "graph")
    return jax.shard_map(
        body,
        mesh=mesh,
        in_specs=(
            P(both, None, None), P(both, None, None), P(None, both), P(both, None),
            P(both), P(both), P(both, None), P(), P(), P(),
        ),
        out_specs=(P(both, None, None), P(both, None), P(both), P(both), P(both)),
        check_vma=False,
    )
```
